32 devices in a mesh: lat: 4 (over z), lon: 8 (over y, x, core).
Axes of the slice: x: 2, y: 2, z: 4, core: 2. Of those that a mesh axis runs over, the one named last changes fastest.
Arguments:
- control: float32 [16, 512, 512], P('lat', 'lon'), may hold values from -1.2 to 1.2
- vert_factor: float32 [4, 128, 128], replicated, may hold values from -0.5 to 0.5
- zonal_factor: float32 [512, 512], replicated, may hold values from -0.25 to 0.25
- obs_dest: int32 [24576, 1], P(('lat', 'lon')), may hold values from 0 to 31; in each aligned block of 768 rows (0 to 767, 768 to 1535, ...) at most 36 rows name the same one
- obs_cell: int32 [24576], P(('lat', 'lon')), may hold values from 0 to 255
- obs_offset: int32 [24576], P(('lat', 'lon')), may hold values from 0 to 96
- obs_count: int32 [32], P(('lat', 'lon')), may hold values from 384 to 768, as said below
- departure: float32 [24576], P(('lat', 'lon')), may hold values from -6 to 6
- obs_rinv: float32 [24576], P(('lat', 'lon')), may hold values from 0.25 to 4
- obs_weights: float32 [24576, 128], P(('lat', 'lon')), may hold values from 0 to 1
Outputs:
- gradient: float32 [16, 512, 512], P('lat', 'lon')
The draws below stay inside these ranges and needn't reach their ends.
Inputs may be any that keep to these rules, and one draw needn't show every extreme that they name: Among the 768 observations of one device, at most 36 have the same obs_dest, and some value is taken exactly 36 times on some devices. `obs_count`: some device holds exactly 768 live observations.
All inputs are finite; a program needn't handle non-finite values.
Results may differ from the reference program's by a relative error of at most 0.000068.
Values sent between devices are 32-bit elements; how exact they have to be, the bound alone decides.
No kernel may reach another device: no remote copies, remote signals or barrier semaphores. Data moves between devices by JAX's collectives and lax.ppermute only.
A program may use at most 64 MiB of HBM per device.

```python
import math
import jax
import jax.numpy as jnp
import numpy as np
from jax import lax

F = 4
LEV = 128
KW = 32
CLAT = 4
CLON = 64
OBS_DEV = 768
NLAT = 16
NLON = 512
NOBS = 24576
CAP = 36
N_LON = 8
DEVICES = 32


def draw_obs_count(key, part):
    key_level = jax.random.fold_in(key, 11)
    key_pick = jax.random.fold_in(key, 13)
    counts = jax.random.randint(key_level, (DEVICES,), OBS_DEV // 2, OBS_DEV + 1)
    chosen = jax.random.randint(key_pick, (), 0, DEVICES)
    return counts.at[chosen].set(OBS_DEV).astype(jnp.int32)


def with_ends(entries, own_key, least, top_value):
    shape = entries.shape
    spot = [jax.random.randint(jax.random.fold_in(own_key, axis), (), 0, shape[axis]) for axis in range(len(shape))]
    entries = entries.at[tuple(spot)].set(least)
    longest = shape.index(max(shape))
    spot[longest] = (spot[longest] + 1) % shape[longest]
    return entries.at[tuple(spot)].set(top_value)


def levels(key, extent, shards, smallest, top_value):
    def one(axis_at, parts):
        draws = jax.random.uniform(jax.random.fold_in(jax.random.fold_in(key, 6), axis_at), (parts,), jnp.float32, smallest / len(shards), top_value / len(shards))
        return jnp.repeat(jnp.exp(draws), extent[axis_at] // parts).reshape((-1,) + (1,) * (len(extent) - axis_at - 1))

    loudness = one(*shards[0])
    for cut in shards[1:]:
        loudness = loudness * one(*cut)
    return loudness


def routed_block(rng, own, number, rows, count, top, most, slope):
    sequence = jax.random.permutation(rng, count)
    packed, ordinary = portions_of(count, rows * top, most, slope, True), portions_of(count, rows * top, most, slope, False)
    places = jnp.arange(count)

    def named(sizes, turn):
        used = int((sizes > 0).sum())
        fixed = max(1, used // 4)
        shifted = fixed + (places - fixed + turn * (used - fixed)) % max(1, count - fixed)
        return jnp.zeros((count,), jnp.int32).at[sequence[jnp.where(places < fixed, places, shifted)]].set(jnp.asarray(sizes, jnp.int32))

    sizes = jnp.where(number % 4 == 0, named(packed, number // 4), named(ordinary, number - number // 4 - 1))
    mixed = jax.random.permutation(jax.random.fold_in(own, 3), count)
    donor, sink = mixed[0:count // 2 * 2:2], mixed[1:count // 2 * 2:2]
    slack = jnp.minimum(sizes[donor] - 1, most - sizes[sink]) // 2
    slack = jnp.where((donor == sequence[0]) | (sink == sequence[0]) | (sizes[sink] == 0), 0, jnp.maximum(slack, 0))
    shifted = jax.random.randint(jax.random.fold_in(own, 4), (count // 2,), 0, 1 << 20) % (slack + 1)
    sizes = sizes.at[donor].add(-shifted).at[sink].add(shifted)
    items = jnp.searchsorted(jnp.cumsum(sizes), jnp.arange(rows * top), side="right").astype(jnp.int32)
    listing = items.reshape(top, rows).T
    listing = listing[jax.random.permutation(jax.random.fold_in(own, 1), rows)]
    turn = jax.random.randint(jax.random.fold_in(own, 2), (rows, 1), 0, top)
    return jnp.take_along_axis(listing, (jnp.arange(top)[None, :] + turn) % top, axis=1)


def portions_of(count, total, limit, slope, full):
    portions = [(1 << 20) // math.isqrt(grade ** slope) + 1 for grade in range(1, count + 1)]
    largest = limit if full else min(limit, max(-(-total // count), total * portions[0] // sum(portions)))
    least = 1 if total - largest >= count - 1 else 0
    holding, rest = [largest] + [least] * (count - 1), total - largest - least * (count - 1)
    while rest > 0:
        free = [i for i in range(1, count) if holding[i] < largest] or [i for i in range(1, count) if holding[i] < limit]
        mass, budget = sum([portions[i] for i in free]), rest
        for i in free:
            addition = min(limit - holding[i], max(1, budget * portions[i] // mass), rest)
            holding[i] = holding[i] + addition
            rest = rest - addition
    return np.array(holding)


def noise(rng, shape, scale, most, split=(), held_as=jnp.bfloat16):
    result = scale * jax.random.normal(rng, shape, jnp.float32)
    if split:
        result = result * levels(rng, shape, split, -0.22, 0.18)
    return jnp.clip(result, -most, most).astype(held_as)


def setup_inputs(seed: int = 0) -> dict:
    key_of = jax.random.split(jax.random.key(seed), 11)
    control = noise(key_of[0], (NLAT, NLON, F * LEV), 0.2, 1.2, ((0, 4), (1, 8)), jnp.float32)
    vert_factor = noise(key_of[1], (F, LEV, LEV), LEV ** -0.5, 0.5, (), jnp.float32)
    zonal_factor = noise(key_of[2], (NLON, NLON), NLON ** -0.5, 0.25, (), jnp.float32)
    obs_dest_keys = jax.random.split(jax.random.fold_in(key_of[3], 1), NOBS // OBS_DEV)
    obs_dest_turns = jax.random.permutation(jax.random.fold_in(key_of[3], 3), NOBS // OBS_DEV)
    obs_dest = jax.vmap(lambda own, number: routed_block(jax.random.fold_in(key_of[3], 2), own, number, OBS_DEV, DEVICES, 1, CAP, 2))(obs_dest_keys, obs_dest_turns).reshape((NOBS, 1))
    obs_cell = with_ends(jax.random.randint(key_of[4], (NOBS,), 0, CLAT * CLON), jax.random.fold_in(key_of[4], 1), 0, (CLAT * CLON) - 1).astype(jnp.int32)
    obs_offset = with_ends(jax.random.randint(key_of[5], (NOBS,), 0, LEV - KW + 1), jax.random.fold_in(key_of[5], 1), 0, LEV - KW).astype(jnp.int32)
    obs_count = draw_obs_count(jax.random.fold_in(key_of[10], 71), 0)
    departure = noise(key_of[7], (NOBS,), 1.0, 6.0, ((0, 32),), jnp.float32)
    obs_rinv = jnp.clip(jnp.exp(math.log(4.0) - 2.7725887 * jax.random.uniform(key_of[8], (NOBS,), jnp.float32) ** levels(key_of[8], (NOBS,), ((0, 32),), -0.2, 0.2)), 0.25, 4.0)
    obs_weights = jnp.clip(1.0 * jax.random.uniform(key_of[9], (NOBS, F * KW), jnp.float32) ** levels(key_of[9], (NOBS, F * KW), ((0, 32),), -0.2, 0.2), 0.0, 1.0)
    return {"control": control, "vert_factor": vert_factor, "zonal_factor": zonal_factor, "obs_dest": obs_dest, "obs_cell": obs_cell, "obs_offset": obs_offset, "obs_count": obs_count, "departure": departure, "obs_rinv": obs_rinv, "obs_weights": obs_weights}


def reference(control, vert_factor, zonal_factor, obs_dest, obs_cell, obs_offset, obs_count, departure, obs_rinv, obs_weights):
    rows = jnp.arange(NOBS, dtype=jnp.int32)
    holder = rows // OBS_DEV
    live = (rows % OBS_DEV) < obs_count[holder]
    scaled = jnp.where(live, obs_rinv * departure, jnp.float32(0.0))
    values = (obs_weights * scaled[:, None]).reshape(NOBS, F, KW)
    dest = obs_dest[:, 0]
    glat = (dest // N_LON) * CLAT + obs_cell // CLON
    glon = (dest % N_LON) * CLON + obs_cell % CLON
    column = (glat * NLON + glon).astype(jnp.int32)
    flat = (column[:, None, None] * (F * LEV)
            + jnp.arange(F, dtype=jnp.int32)[None, :, None] * LEV
            + obs_offset[:, None, None]
            + jnp.arange(KW, dtype=jnp.int32)[None, None, :]).astype(jnp.int32)
    adjoint = jnp.zeros((NLAT * NLON * F * LEV,), jnp.float32).at[flat.reshape(-1)].add(values.reshape(-1))
    adjoint = adjoint.reshape(NLAT, NLON, F, LEV)

    def one_row(pair):
        block, base = pair
        vertical = jnp.einsum("nfk,fkl->nfl", block, vert_factor, precision=lax.Precision.HIGHEST)
        zonal = jnp.einsum("nfl,nm->mfl", vertical, zonal_factor, precision=lax.Precision.HIGHEST)
        return base + zonal.reshape(NLON, F * LEV)

    return lax.map(one_row, (adjoint, control))
```

```python
import functools

import jax
import jax.numpy as jnp
from jax import lax
from jax.experimental import pallas as pl
from jax.experimental.pallas import tpu as pltpu
from jax.sharding import PartitionSpec as P

F = 4
LEV = 128
KW = 32
LANES = 128
SUBLANES = 8
GROUPS = LANES // KW
MIB = 1 << 20


def iota(shape, axis):
    return lax.broadcasted_iota(jnp.int32, shape, axis)


def split(x):
    high = x.astype(jnp.bfloat16)
    return high, (x - high.astype(jnp.float32)).astype(jnp.bfloat16)


def dot(a, b):
    return jnp.dot(a, b, preferred_element_type=jnp.float32)


def call(kernel, out_shape, n_in, smem=(), vmem=24, flops=0, nbytes=0, scratch=()):
    specs = [
        pl.BlockSpec(memory_space=pltpu.SMEM if i in smem else pltpu.VMEM) for i in range(n_in)
    ]
    one = pl.BlockSpec(memory_space=pltpu.VMEM)
    return pl.pallas_call(
        kernel,
        out_shape=out_shape,
        in_specs=specs,
        out_specs=[one] * len(out_shape) if isinstance(out_shape, (list, tuple)) else one,
        scratch_shapes=list(scratch),
        compiler_params=pltpu.CompilerParams(vmem_limit_bytes=vmem * MIB),
        cost_estimate=pl.CostEstimate(flops=flops, bytes_accessed=nbytes, transcendentals=0),
    )


def message_rows(capacity):
    parts = -(-capacity // KW)
    return parts, -(-(capacity + 2 * parts) // SUBLANES) * SUBLANES


def pack_kernel(
    lons, members, capacity, count, dest, cell, offset, departure, rinv, weights, out, picked
):
    n = weights.shape[0]
    devices = out.shape[0]
    rows = out.shape[1]
    parts, _ = message_rows(capacity)
    quads = devices // GROUPS
    chunks = n // LANES
    dest_row = dest[...]
    hits = [
        iota((devices, LANES), 0) == dest_row[:, c * LANES : (c + 1) * LANES] for c in range(chunks)
    ]
    stacked = jnp.concatenate([hit.astype(jnp.bfloat16) for hit in hits], axis=0)
    before = (iota((LANES, 2 * LANES), 0) < iota((LANES, 2 * LANES), 1)).astype(jnp.bfloat16)
    counts = dot(stacked, before)
    carry = jnp.zeros((devices, LANES), jnp.float32)
    ranks = []
    for c in range(chunks):
        part = counts[c * devices : (c + 1) * devices]
        ranks.append(
            jnp.sum(jnp.where(hits[c], part[:, :LANES] + carry, 0.0), axis=0, keepdims=True)
        )
        carry = carry + part[:, LANES:]
    rank = jnp.concatenate(ranks, axis=1).astype(jnp.int32)
    position = dest_row * rows + rank
    group = dest_row & (GROUPS - 1)
    quad = dest_row >> (GROUPS.bit_length() - 1)
    lane = group * KW + (rank & (KW - 1))
    piece = rank >> (KW.bit_length() - 1)
    live = iota((1, n), 1) < count[0]
    scaled = jnp.where(live, rinv[...] * departure[...], jnp.float32(0.0))
    columns = jnp.concatenate(
        [
            scaled,
            lane.astype(jnp.float32),
            offset[...].astype(jnp.float32),
            jnp.zeros((SUBLANES - 3, n), jnp.float32),
        ],
        axis=0,
    ).T
    lane_id = iota((n, LANES), 1)
    source = (lane_id & -KW) | ((lane_id - columns[:, 2:3].astype(jnp.int32)) & (KW - 1))
    turned = jnp.take_along_axis(weights[...], source, axis=1, mode="promise_in_bounds")
    high, low = split(turned * columns[:, 0:1])
    lane_hit = (columns[:, 1:2].astype(jnp.int32) == lane_id).astype(jnp.bfloat16)
    label_rows = []
    for p in range(parts):
        for label in (cell, offset):
            mine = (iota((quads, n), 0) == quad) & (piece == p)
            label_rows.append(jnp.where(mine, label[...].astype(jnp.float32), 0.0))
    labels = dot(jnp.concatenate(label_rows, axis=0).astype(jnp.bfloat16), lane_hit)
    slot_hit = (iota((devices * rows, n), 0) == position).astype(jnp.bfloat16)
    both = dot(slot_hit, jnp.concatenate([high, low], axis=1))
    picked[...] = both[:, :LANES] + both[:, LANES:]
    lane_group = iota((rows, LANES), 1) >> (KW.bit_length() - 1)
    row_id = iota((rows, LANES), 0)
    for q in range(quads):
        band, member = q // members, q % members
        extra = jnp.zeros((rows, LANES), jnp.float32)
        for k in range(2 * parts):
            extra = jnp.where(row_id == capacity + k, labels[k * quads + q : k * quads + q + 1], extra)
        blocks = [
            picked[(q * GROUPS + g) * rows : (q * GROUPS + g + 1) * rows, :] for g in range(GROUPS)
        ]
        for f in range(F):
            message = extra
            for g in range(GROUPS):
                turned = blocks[g]
                if g != f:
                    turned = pltpu.roll(turned, (KW * (g - f)) % LANES, 1)
                message = jnp.where((lane_group == g) & (row_id < capacity), turned, message)
            out[band * lons + f * members + member] = message


def prepare_kernel(members, lon_cols, place, zonal, vert, zonal_high, zonal_low, vert_both, turned):
    f, h = place[0], place[1]
    width = GROUPS * lon_cols
    turned[...] = zonal[...].T
    for q in range(F):
        row = pl.multiple_of(((f ^ q) * members + h) * lon_cols, lon_cols)
        for e in range(members):
            source = lax.rem(h + members - e, members)
            part = turned[pl.ds(row, lon_cols), pl.ds(pl.multiple_of(source * width, LANES), width)]
            high, low = split(part)
            zonal_high[q * lon_cols : (q + 1) * lon_cols, e * width : (e + 1) * width] = high
            zonal_low[q * lon_cols : (q + 1) * lon_cols, e * width : (e + 1) * width] = low
    high, low = split(vert[f])
    vert_both[:, :LEV] = high
    vert_both[:, LEV:] = low


def place_kernel(capacity, lon_cols, received, vert_both, out):
    devices, rows, _ = received.shape
    parts, _ = message_rows(capacity)
    slots = devices * rows
    columns = out.shape[1] // LEV * lon_cols
    high, low = split(received[...].reshape(slots, LANES))
    row_id, lane_id = iota((rows, LANES), 0), iota((rows, LANES), 1)
    diagonal = (lane_id & (KW - 1)) == (row_id & (KW - 1))
    cells = jnp.where((row_id >= capacity) & ((lane_id & (KW - 1)) == 0), -1.0, 0.0)[None]
    offsets = jnp.zeros((1, rows, LANES), jnp.float32)
    for p in range(parts):
        mine = (diagonal & (row_id >> (KW.bit_length() - 1) == p) & (row_id < capacity))[None]
        at = capacity + 2 * p
        cells = jnp.where(mine, received[:, at : at + 1, :], cells)
        offsets = jnp.where(mine, received[:, at + 1 : at + 2, :], offsets)
    cells = cells.reshape(slots, LANES).astype(jnp.bfloat16)
    offsets = offsets.reshape(slots, LANES).astype(jnp.bfloat16)
    wide = (LANES, GROUPS * LEV)
    spread = (iota(wide, 0) >> 5 == iota(wide, 1) >> 7).astype(jnp.bfloat16)
    tile = (
        (iota(wide, 0) >> 5 == iota(wide, 1) >> 7) & ((iota(wide, 0) & 31) == (iota(wide, 1) & 31))
    ).astype(jnp.bfloat16)
    picker = (iota((SUBLANES, LANES), 0) == iota((SUBLANES, LANES), 1) >> 5).astype(jnp.bfloat16)
    cell_rows = lax.dot_general(
        picker, cells, (((1,), (1,)), ((), ())), preferred_element_type=jnp.float32
    ).astype(jnp.int32)
    middle = iota((slots, LEV), 1).astype(jnp.float32) - (KW - 1) / 2
    for g in range(GROUPS):
        part = slice(g * LEV, (g + 1) * LEV)
        inside = jnp.abs(middle - dot(offsets, spread[:, part])) < KW / 2
        placed = jnp.concatenate(
            [
                jnp.where(inside, dot(high, tile[:, part]), 0.0).astype(jnp.bfloat16),
                jnp.where(inside, dot(low, tile[:, part]), 0.0).astype(jnp.bfloat16),
            ],
            axis=1,
        )
        hit = (iota((columns, slots), 0) == cell_rows[g : g + 1]).astype(jnp.bfloat16)
        both = dot(hit, placed)
        adjoint_high, adjoint_low = split(both[:, :LEV] + both[:, LEV:])
        first = dot(adjoint_high, vert_both[...])
        vertical = first[:, :LEV] + first[:, LEV:] + dot(adjoint_low, vert_both[:, :LEV])
        for a in range(columns // lon_cols):
            out[g * lon_cols : (g + 1) * lon_cols, a * LEV : (a + 1) * LEV] = vertical[
                a * lon_cols : (a + 1) * lon_cols
            ]


def zonal_term(e, width, zonal_high, zonal_low, vertical):
    part = slice(e * width, (e + 1) * width)
    high, low = split(vertical[...])
    first = dot(zonal_high[:, part], high) + dot(zonal_low[:, part], high)
    return first + dot(zonal_high[:, part], low)


def own_kernel(zonal_high, zonal_low, vertical, out):
    out[...] = zonal_term(0, vertical.shape[0], zonal_high, zonal_low, vertical)


def zonal_kernel(members, lon_cols, *refs):
    zonal_high, zonal_low, total = refs[:3]
    verticals, outs = refs[3 : 2 + members], refs[2 + members :]
    product = total[...]
    for e, vertical in enumerate(verticals, 1):
        product = product + zonal_term(e, vertical.shape[0], zonal_high, zonal_low, vertical)
    for q in range(F):
        outs[q][...] = product[q * lon_cols : (q + 1) * lon_cols]


def finish_kernel(place, control, *refs):
    parts, out = refs[:F], refs[F]
    for q in range(F):
        at = pl.ds(pl.multiple_of((place[0] ^ q) * LEV, LEV), LEV)
        for a in range(control.shape[0]):
            out[a, :, at] = control[a, :, at] + parts[q][:, a * LEV : (a + 1) * LEV]


def per_device(
    control,
    vert_factor,
    zonal_factor,
    obs_dest,
    obs_cell,
    obs_offset,
    obs_count,
    departure,
    obs_rinv,
    obs_weights,
):
    lats = lax.axis_size("lat")
    lons = lax.axis_size("lon")
    devices = lats * lons
    members = lons // F
    n_obs = obs_cell.shape[0]
    capacity = max(2, 3 * n_obs // (2 * devices))
    _, rows = message_rows(capacity)
    lat_rows, lon_cols, _ = control.shape
    width = GROUPS * lon_cols
    wide = lat_rows * LEV
    f32, bf16 = jnp.float32, jnp.bfloat16
    position = lax.axis_index("lon").astype(jnp.int32)
    place = jnp.stack([position // members, position % members])
    messages = call(
        functools.partial(pack_kernel, lons, members, capacity),
        jax.ShapeDtypeStruct((devices, rows, LANES), f32),
        7,
        smem=(0,),
        scratch=[pltpu.VMEM((devices * rows, LANES), f32)],
        flops=4 * devices * rows * n_obs * LANES,
        nbytes=1 << 20,
    )(
        obs_count,
        obs_dest.reshape(1, n_obs),
        obs_cell.reshape(1, n_obs),
        obs_offset.reshape(1, n_obs),
        departure.reshape(1, n_obs),
        obs_rinv.reshape(1, n_obs),
        obs_weights,
    )
    received = lax.all_to_all(messages, ("lat", "lon"), 0, 0, tiled=True)
    zonal_high, zonal_low, vert_both = call(
        functools.partial(prepare_kernel, members, lon_cols),
        [
            jax.ShapeDtypeStruct((F * lon_cols, members * width), bf16),
            jax.ShapeDtypeStruct((F * lon_cols, members * width), bf16),
            jax.ShapeDtypeStruct((LEV, 2 * LEV), bf16),
        ],
        3,
        smem=(0,),
        scratch=[pltpu.VMEM(zonal_factor.shape, f32)],
        nbytes=2 << 20,
    )(place, zonal_factor, vert_factor)
    vertical = call(
        functools.partial(place_kernel, capacity, lon_cols),
        jax.ShapeDtypeStruct((width, wide), f32),
        2,
        vmem=32,
        flops=16 * devices * rows * lat_rows * width * LEV,
        nbytes=2 << 20,
    )(received, vert_both)
    others = [
        lax.ppermute(
            vertical,
            "lon",
            [
                (i, i // members * members + (i % members + e) % members)
                for i in range(lons)
            ],
        )
        for e in range(1, members)
    ]
    total = call(
        own_kernel,
        jax.ShapeDtypeStruct((F * lon_cols, wide), f32),
        3,
        flops=6 * F * lon_cols * width * wide,
        nbytes=1 << 20,
    )(zonal_high, zonal_low, vertical)
    blocks = call(
        functools.partial(zonal_kernel, members, lon_cols),
        [jax.ShapeDtypeStruct((lon_cols, wide), f32)] * F,
        2 + members,
        flops=6 * F * lon_cols * width * wide,
        nbytes=1 << 20,
    )(zonal_high, zonal_low, total, *others)
    parts = [blocks[0]] + [
        lax.ppermute(
            blocks[q],
            "lon",
            [(i, (i // members ^ q) * members + i % members) for i in range(lons)],
        )
        for q in range(1, F)
    ]
    return call(
        finish_kernel,
        jax.ShapeDtypeStruct(control.shape, f32),
        2 + F,
        smem=(0,),
        nbytes=2 << 20,
    )(place, control, *parts)


def solution(mesh):
    return jax.shard_map(
        per_device,
        mesh=mesh,
        in_specs=(
            P("lat", "lon", None),
            P(),
            P(),
            P(("lat", "lon"), None),
            P(("lat", "lon")),
            P(("lat", "lon")),
            P(("lat", "lon")),
            P(("lat", "lon")),
            P(("lat", "lon")),
            P(("lat", "lon"), None),
        ),
        out_specs=P("lat", "lon", None),
        check_vma=False,
    )
```

```python
import functools

import jax
import jax.numpy as jnp
from jax import lax
from jax.experimental import pallas as pl
from jax.experimental.pallas import tpu as pltpu
from jax.sharding import PartitionSpec as P

F = 4
LEV = 128
KW = 32
LANES = 128
SUBLANES = 8
GROUPS = LANES // KW
NEAR = 2
MIB = 1 << 20


def iota(shape, axis):
    return lax.broadcasted_iota(jnp.int32, shape, axis)


def split(x):
    high = x.astype(jnp.bfloat16)
    return high, (x - high.astype(jnp.float32)).astype(jnp.bfloat16)


def dot(a, b):
    return jnp.dot(a, b, preferred_element_type=jnp.float32)


def one_hot(labels, size):
    hit = iota((size, labels.shape[1]), 0).astype(jnp.bfloat16) == labels.astype(jnp.bfloat16)
    return jnp.where(hit, jnp.bfloat16(1), jnp.bfloat16(0))


def message_rows(capacity):
    parts = -(-capacity // KW)
    return parts, -(-(capacity + 2 * parts) // SUBLANES) * SUBLANES


def pack_kernel(members, capacity, lats, *refs):
    sources, far, near = refs[:7], refs[7 : 7 + F], refs[7 + F : 7 + F + NEAR]
    held, arrived = refs[7 + F + NEAR : -1], refs[-1]
    loads = [
        pltpu.make_async_copy(source, target, arrived.at[i])
        for i, (source, target) in enumerate(zip(sources, held))
    ]
    for load in loads:
        load.start()
    count, dest, cell, offset, departure, rinv, weights = held
    n = weights.shape[0]
    rows = far[0].shape[2]
    lons = F * members
    devices = lats * lons
    field = lax.axis_index("lon") // members
    parts, _ = message_rows(capacity)
    quads = devices // GROUPS
    chunks = n // LANES
    loads[1].wait()
    dest_row = dest[...] ^ (lax.axis_index("lat") * lons)
    hits = [
        iota((devices, LANES), 0) == dest_row[:, c * LANES : (c + 1) * LANES] for c in range(chunks)
    ]
    stacked = jnp.concatenate([hit.astype(jnp.bfloat16) for hit in hits], axis=0)
    before = (iota((LANES, 2 * LANES), 0) < iota((LANES, 2 * LANES), 1)).astype(jnp.bfloat16)
    counts = dot(stacked, before)
    carry = jnp.zeros((devices, LANES), jnp.float32)
    ranks = []
    for c in range(chunks):
        part = counts[c * devices : (c + 1) * devices]
        ranks.append(
            jnp.sum(jnp.where(hits[c], part[:, :LANES] + carry, 0.0), axis=0, keepdims=True)
        )
        carry = carry + part[:, LANES:]
    rank = jnp.concatenate(ranks, axis=1).astype(jnp.int32)
    group = dest_row & (GROUPS - 1)
    quad = dest_row >> (GROUPS.bit_length() - 1)
    slot = group * rows + rank
    lane = group * KW + (rank & (KW - 1))
    piece = rank >> (KW.bit_length() - 1)
    for i in (0, 2, 3, 4, 5):
        loads[i].wait()
    cell_row, offset_row = cell[...].reshape(1, n), offset[...].reshape(1, n)
    live = iota((1, n), 1) < count[0, 0]
    scaled = jnp.where(
        live, rinv[...].reshape(1, n) * departure[...].reshape(1, n), jnp.float32(0.0)
    )
    columns = jnp.concatenate(
        [
            scaled,
            lane.astype(jnp.float32),
            offset_row.astype(jnp.float32),
            jnp.zeros((SUBLANES - 3, n), jnp.float32),
        ],
        axis=0,
    ).T
    lane_id = iota((n, LANES), 1)
    lane_hit = (columns[:, 1:2].astype(jnp.int32) == lane_id).astype(jnp.bfloat16)
    label_rows = []
    for p in range(parts):
        for label in (cell_row, offset_row):
            mine = (iota((quads, n), 0) == quad) & (piece == p)
            label_rows.append(jnp.where(mine, label.astype(jnp.float32), 0.0))
    labels = dot(jnp.concatenate(label_rows, axis=0).astype(jnp.bfloat16), lane_hit)
    source = (lane_id & -KW) | ((lane_id - columns[:, 2:3].astype(jnp.int32)) & (KW - 1))
    loads[6].wait()
    turned = jnp.take_along_axis(weights[...], source, axis=1, mode="promise_in_bounds")
    high, low = split(turned * columns[:, 0:1])
    pieces = jnp.concatenate([high, low], axis=1)
    lane_group = iota((rows, LANES), 1) >> (KW.bit_length() - 1)
    row_id = iota((rows, LANES), 0)
    for distance in (*range(NEAR, lats), *reversed(range(NEAR))):
        for half in range(members):
            at = distance * members + half
            extra = jnp.zeros((rows, LANES), jnp.float32)
            for i in range(2 * parts):
                label = labels[i * quads + at : i * quads + at + 1]
                extra = jnp.where(row_id == capacity + i, label, extra)
            slot_hit = one_hot(jnp.where(quad == at, slot, -1), GROUPS * rows)
            both = dot(slot_hit, pieces)
            picked = both[:, :LANES] + both[:, LANES:]
            for q in range(F):
                message = extra
                for g in range(GROUPS):
                    shift = (KW * (g - (field ^ q))) & (LANES - 1)
                    turned = pltpu.roll(picked[g * rows : (g + 1) * rows], shift, 1)
                    message = jnp.where((lane_group == g) & (row_id < capacity), turned, message)
                if distance < NEAR:
                    near[distance][q, half] = message
                else:
                    far[q][distance - NEAR, half] = message


def prepare_kernel(members, lon_cols, zonal, vert, zonal_high, zonal_low, vert_both, turned):
    position = lax.axis_index("lon")
    f, h = position // members, lax.rem(position, members)
    turned[...] = zonal[...].T
    for e in range(members):
        for q in range(F):
            block = (f ^ q) * members + lax.rem(h + e, members)
            part = turned[pl.ds(pl.multiple_of(block * lon_cols, lon_cols), lon_cols), :]
            at = slice((e * F + q) * lon_cols, (e * F + q + 1) * lon_cols)
            zonal_high[at], zonal_low[at] = split(part)
    high, low = split(vert[f])
    vert_both[:, :LEV] = high
    vert_both[:, LEV:] = low


def scatter(pieces, half, capacity, columns):
    rows = pieces[0].shape[0]
    count = len(pieces)
    slots = -(-count * rows // LANES) * LANES
    parts, _ = message_rows(capacity)
    row_id, lane_id = iota((rows, LANES), 0), iota((rows, LANES), 1)
    piece_id = row_id >> (KW.bit_length() - 1)
    diagonal = ((lane_id & (KW - 1)) == (row_id & (KW - 1))) & (row_id < capacity)
    empty = jnp.where((row_id >= capacity) & ((lane_id & (KW - 1)) == 0), -1.0, 0.0)
    cells, offsets = [], []
    for piece in pieces:
        cell, offset = empty, jnp.zeros((rows, LANES), jnp.float32)
        for p in range(parts):
            mine = diagonal & (piece_id == p)
            at = capacity + 2 * p
            cell = jnp.where(mine, piece[at : at + 1], cell)
            offset = jnp.where(mine, piece[at + 1 : at + 2], offset)
        cells.append(cell)
        offsets.append(offset)
    spare = slots - count * rows
    if spare:
        pieces = pieces + [jnp.zeros((spare, LANES), jnp.float32)]
        cells.append(jnp.full((spare, LANES), -1.0, jnp.float32))
        offsets.append(jnp.zeros((spare, LANES), jnp.float32))
    values = jnp.concatenate(pieces, axis=0)
    cells = jnp.concatenate(cells, axis=0).astype(jnp.bfloat16)
    offsets = jnp.concatenate(offsets, axis=0).astype(jnp.bfloat16)
    wide = (LANES, GROUPS * LEV)
    spread = (
        iota(wide, 0) >> (KW.bit_length() - 1) == iota(wide, 1) >> (LEV.bit_length() - 1)
    ).astype(jnp.bfloat16)
    picker = (
        iota((SUBLANES, LANES), 0) == iota((SUBLANES, LANES), 1) >> (KW.bit_length() - 1)
    ).astype(jnp.bfloat16)
    cell_rows = lax.dot_general(
        picker, cells, (((1,), (1,)), ((), ())), preferred_element_type=jnp.float32
    )
    middle = iota((slots, LEV), 1).astype(jnp.float32) - (KW - 1) / 2
    sums = []
    for g in range(GROUPS):
        if g % 2 == 0:
            starts = dot(offsets, spread[:, g * LEV : (g + 2) * LEV])
        inside = jnp.abs(middle - starts[:, (g % 2) * LEV : (g % 2 + 1) * LEV]) < KW / 2
        source = g * KW + (iota((slots, LANES), 1) & (KW - 1))
        tiled = jnp.take_along_axis(values, source, axis=1, mode="promise_in_bounds")
        placed = jnp.concatenate(split(jnp.where(inside, tiled, 0.0)), axis=1)
        both = dot(one_hot(cell_rows[g : g + 1], columns), placed)
        sums.append(both[:, :LEV] + both[:, LEV:])
    return sums


def early_kernel(capacity, *refs):
    received, out = refs[:-1], refs[-1]
    halves, columns = received[0].shape[1], out.shape[1]
    for half in range(halves):
        pieces = [ref[k, half] for ref in received for k in range(ref.shape[0])]
        for g, total in enumerate(scatter(pieces, half, capacity, columns)):
            out[half * GROUPS + g] = total


def late_kernel(capacity, lon_cols, count, *refs):
    received = refs[:count]
    early, zonal_high, zonal_low, vert_both, high_out, low_out, *partials = refs[count:]
    halves, columns = received[0].shape[1], early.shape[1]
    for half in range(halves):
        pieces = [ref[k, half] for ref in received for k in range(ref.shape[0])]
        for g, total in enumerate(scatter(pieces, half, capacity, columns)):
            block = half * GROUPS + g
            adjoint_high, adjoint_low = split(early[block] + total)
            first = dot(adjoint_high, vert_both[...])
            vertical = first[:, :LEV] + first[:, LEV:] + dot(adjoint_low, vert_both[:, :LEV])
            high, low = split(vertical)
            for a in range(columns // lon_cols):
                at = slice(block * lon_cols, (block + 1) * lon_cols)
                rows = slice(a * lon_cols, (a + 1) * lon_cols)
                high_out[at, a * LEV : (a + 1) * LEV] = high[rows]
                low_out[at, a * LEV : (a + 1) * LEV] = low[rows]
    for e, partial in enumerate(partials, 1):
        partial[...] = zonal_product(e, zonal_high, zonal_low, high_out, low_out, partial.shape[0])


def zonal_product(e, zonal_high, zonal_low, high, low, size):
    at = slice(e * size, (e + 1) * size)
    first = dot(zonal_high[at], high[...]) + dot(zonal_low[at], high[...])
    return first + dot(zonal_high[at], low[...])


def own_kernel(zonal_high, zonal_low, high, low, out):
    out[...] = zonal_product(0, zonal_high, zonal_low, high, low, out.shape[0])


def sum_kernel(lon_cols, *refs):
    terms, outs = refs[:-F], refs[-F:]
    for q in range(F):
        at = slice(q * lon_cols, (q + 1) * lon_cols)
        total = terms[0][at]
        for term in terms[1:]:
            total = total + term[at]
        outs[q][...] = total


def finish_kernel(members, control, *refs):
    parts, out = refs[:F], refs[F]
    field = lax.axis_index("lon") // members
    for q in range(F):
        at = pl.ds(pl.multiple_of((field ^ q) * LEV, LEV), LEV)
        for a in range(control.shape[0]):
            out[a, :, at] = control[a, :, at] + parts[q][:, a * LEV : (a + 1) * LEV]


def call(kernel, out_shape, n_in, vmem=24, flops=0, nbytes=0, scratch=()):
    one = pl.BlockSpec(memory_space=pltpu.VMEM)
    return pl.pallas_call(
        kernel,
        out_shape=out_shape,
        in_specs=[one] * n_in,
        out_specs=[one] * len(out_shape) if isinstance(out_shape, (list, tuple)) else one,
        scratch_shapes=list(scratch),
        compiler_params=pltpu.CompilerParams(vmem_limit_bytes=vmem * MIB),
        cost_estimate=pl.CostEstimate(flops=flops, bytes_accessed=nbytes, transcendentals=0),
    )


def along_lat(x, d):
    lats = lax.axis_size("lat")
    return lax.ppermute(x, "lat", [(i, i ^ d) for i in range(lats)])


def to_field(x, q, members):
    if q == 0:
        return x
    lons = lax.axis_size("lon")
    return lax.ppermute(
        x, "lon", [(i, (i // members ^ q) * members + i % members) for i in range(lons)]
    )


def to_member(x, e, members):
    lons = lax.axis_size("lon")
    return lax.ppermute(
        x, "lon", [(i, i // members * members + (i + e) % members) for i in range(lons)]
    )


def per_device(
    control,
    vert_factor,
    zonal_factor,
    obs_dest,
    obs_cell,
    obs_offset,
    obs_count,
    departure,
    obs_rinv,
    obs_weights,
):
    lats = lax.axis_size("lat")
    lons = lax.axis_size("lon")
    devices = lats * lons
    members = lons // F
    n_obs = obs_cell.shape[0]
    capacity = max(2, 3 * n_obs // (2 * devices))
    _, rows = message_rows(capacity)
    lat_rows, lon_cols, _ = control.shape
    columns = lat_rows * lon_cols
    blocks = lons
    all_lons = lons * lon_cols
    share = F * lon_cols
    wide = lat_rows * LEV
    f32, bf16 = jnp.float32, jnp.bfloat16
    far_messages = jax.ShapeDtypeStruct((lats - NEAR, members, rows, LANES), f32)
    near_messages = jax.ShapeDtypeStruct((F, members, rows, LANES), f32)
    messages = pl.pallas_call(
        functools.partial(pack_kernel, members, capacity, lats),
        out_shape=[far_messages] * F + [near_messages] * NEAR,
        in_specs=[pl.BlockSpec(memory_space=pltpu.HBM)] * 7,
        out_specs=[pl.BlockSpec(memory_space=pltpu.VMEM)] * (F + NEAR),
        scratch_shapes=[
            pltpu.SMEM((1, 1), jnp.int32),
            pltpu.VMEM((1, n_obs), jnp.int32),
            pltpu.VMEM((n_obs,), jnp.int32),
            pltpu.VMEM((n_obs,), jnp.int32),
            pltpu.VMEM((n_obs,), f32),
            pltpu.VMEM((n_obs,), f32),
            pltpu.VMEM((n_obs, LANES), f32),
            pltpu.SemaphoreType.DMA((7,)),
        ],
        compiler_params=pltpu.CompilerParams(vmem_limit_bytes=24 * MIB),
        cost_estimate=pl.CostEstimate(
            flops=4 * devices * rows * n_obs * LANES, bytes_accessed=1 << 20, transcendentals=0
        ),
    )(
        obs_count.reshape(1, 1),
        *(
            pltpu.with_memory_space_constraint(x, pltpu.HBM)
            for x in (
                obs_dest.reshape(1, n_obs),
                obs_cell,
                obs_offset,
                departure,
                obs_rinv,
                obs_weights,
            )
        )
    )
    far = [to_field(messages[q], q, members) for q in range(F)]
    late = [
        along_lat(jnp.stack([part[k] for part in far]), d) for k, d in enumerate(range(NEAR, lats))
    ]
    near = [messages[F]] + [along_lat(messages[F + d], d) for d in range(1, NEAR)]
    near = [to_field(jnp.stack([part[q] for part in near]), q, members) for q in range(F)]
    zonal_high, zonal_low, vert_both = call(
        functools.partial(prepare_kernel, members, lon_cols),
        [
            jax.ShapeDtypeStruct((members * share, all_lons), bf16),
            jax.ShapeDtypeStruct((members * share, all_lons), bf16),
            jax.ShapeDtypeStruct((LEV, 2 * LEV), bf16),
        ],
        2,
        scratch=[pltpu.VMEM(zonal_factor.shape, f32)],
        nbytes=2 << 20,
    )(zonal_factor, vert_factor)
    early = call(
        functools.partial(early_kernel, capacity),
        jax.ShapeDtypeStruct((blocks, columns, LEV), f32),
        F,
        vmem=24,
        flops=4 * blocks * columns * NEAR * F * rows * LEV,
        nbytes=2 << 20,
    )(*near)
    partial = jax.ShapeDtypeStruct((share, wide), f32)
    half_vertical = jax.ShapeDtypeStruct((all_lons, wide), bf16)
    high, low, *partials = call(
        functools.partial(late_kernel, capacity, lon_cols, len(late)),
        [half_vertical] * 2 + [partial] * (members - 1),
        4 + len(late),
        vmem=24,
        flops=6 * members * share * all_lons * wide,
        nbytes=2 << 20,
    )(*late, early, zonal_high, zonal_low, vert_both)
    others = [to_member(partials[e - 1], e, members) for e in range(1, members)]
    own = call(
        own_kernel, partial, 4, flops=6 * share * all_lons * wide, nbytes=1 << 20
    )(zonal_high, zonal_low, high, low)
    products = call(
        functools.partial(sum_kernel, lon_cols),
        [jax.ShapeDtypeStruct((lon_cols, wide), f32)] * F,
        members,
        nbytes=1 << 20,
    )(own, *others)
    parts = [to_field(products[q], q, members) for q in range(F)]
    return call(
        functools.partial(finish_kernel, members),
        jax.ShapeDtypeStruct(control.shape, f32),
        1 + F,
        nbytes=2 << 20,
    )(control, *parts)


def solution(mesh):
    return jax.shard_map(
        per_device,
        mesh=mesh,
        in_specs=(
            P("lat", "lon", None),
            P(),
            P(),
            P(("lat", "lon"), None),
            P(("lat", "lon")),
            P(("lat", "lon")),
            P(("lat", "lon")),
            P(("lat", "lon")),
            P(("lat", "lon")),
            P(("lat", "lon"), None),
        ),
        out_specs=P("lat", "lon", None),
        check_vma=False,
    )
```

```python
import functools

import jax
import jax.numpy as jnp
from jax import lax
from jax.experimental import pallas as pl
from jax.experimental.pallas import tpu as pltpu
from jax.sharding import PartitionSpec as P

F = 4
LEV = 128
KW = 32
LANES = 128
SUBLANES = 8
GROUPS = LANES // KW
NEAR = 2
MIB = 1 << 20


def iota(shape, axis):
    return lax.broadcasted_iota(jnp.int32, shape, axis)


def split(x):
    high = x.astype(jnp.bfloat16)
    return high, (x - high.astype(jnp.float32)).astype(jnp.bfloat16)


def dot(a, b):
    return jnp.dot(a, b, preferred_element_type=jnp.float32)


def one_hot(labels, size):
    hit = iota((size, labels.shape[1]), 0).astype(jnp.bfloat16) == labels.astype(jnp.bfloat16)
    return jnp.where(hit, jnp.bfloat16(1), jnp.bfloat16(0))


def message_rows(capacity):
    parts = -(-capacity // KW)
    return parts, -(-(capacity + 2 * parts) // SUBLANES) * SUBLANES


def pack_kernel(members, capacity, lats, *refs):
    sources, far, near = refs[:7], refs[7 : 7 + F], refs[7 + F : 7 + F + NEAR]
    held, arrived = refs[7 + F + NEAR : -1], refs[-1]
    loads = [
        pltpu.make_async_copy(source, target, arrived.at[i])
        for i, (source, target) in enumerate(zip(sources, held))
    ]
    for load in loads:
        load.start()
    count, dest, cell, offset, departure, rinv, weights = held
    n = weights.shape[0]
    rows = far[0].shape[2]
    lons = F * members
    devices = lats * lons
    field = lax.axis_index("lon") // members
    parts, _ = message_rows(capacity)
    quads = devices // GROUPS
    chunks = n // LANES
    loads[1].wait()
    lat = lax.axis_index("lat")
    band = dest[...] // lons ^ lat
    dest_row = (band ^ ((band & lat & 2) >> 1)) * lons + lax.rem(dest[...], lons)
    hits = [
        iota((devices, LANES), 0) == dest_row[:, c * LANES : (c + 1) * LANES] for c in range(chunks)
    ]
    stacked = jnp.concatenate([hit.astype(jnp.bfloat16) for hit in hits], axis=0)
    before = (iota((LANES, 2 * LANES), 0) < iota((LANES, 2 * LANES), 1)).astype(jnp.bfloat16)
    counts = dot(stacked, before)
    carry = jnp.zeros((devices, LANES), jnp.float32)
    ranks = []
    for c in range(chunks):
        part = counts[c * devices : (c + 1) * devices]
        ranks.append(
            jnp.sum(jnp.where(hits[c], part[:, :LANES] + carry, 0.0), axis=0, keepdims=True)
        )
        carry = carry + part[:, LANES:]
    rank = jnp.concatenate(ranks, axis=1).astype(jnp.int32)
    group = dest_row & (GROUPS - 1)
    quad = dest_row >> (GROUPS.bit_length() - 1)
    slot = group * rows + rank
    lane = group * KW + (rank & (KW - 1))
    piece = rank >> (KW.bit_length() - 1)
    for i in (0, 2, 3, 4, 5):
        loads[i].wait()
    cell_row, offset_row = cell[...].reshape(1, n), offset[...].reshape(1, n)
    live = iota((1, n), 1) < count[0, 0]
    scaled = jnp.where(
        live, rinv[...].reshape(1, n) * departure[...].reshape(1, n), jnp.float32(0.0)
    )
    columns = jnp.concatenate(
        [
            scaled,
            lane.astype(jnp.float32),
            offset_row.astype(jnp.float32),
            jnp.zeros((SUBLANES - 3, n), jnp.float32),
        ],
        axis=0,
    ).T
    lane_id = iota((n, LANES), 1)
    lane_hit = (columns[:, 1:2].astype(jnp.int32) == lane_id).astype(jnp.bfloat16)
    label_rows = []
    for p in range(parts):
        for label in (cell_row, offset_row):
            mine = (iota((quads, n), 0) == quad) & (piece == p)
            label_rows.append(jnp.where(mine, label.astype(jnp.float32), 0.0))
    labels = dot(jnp.concatenate(label_rows, axis=0).astype(jnp.bfloat16), lane_hit)
    source = (lane_id & -KW) | ((lane_id - columns[:, 2:3].astype(jnp.int32)) & (KW - 1))
    loads[6].wait()
    turned = jnp.take_along_axis(weights[...], source, axis=1, mode="promise_in_bounds")
    high, low = split(turned * columns[:, 0:1])
    pieces = jnp.concatenate([high, low], axis=1)
    lane_group = iota((rows, LANES), 1) >> (KW.bit_length() - 1)
    row_id = iota((rows, LANES), 0)
    size = GROUPS * rows
    order = (*range(NEAR, lats), *reversed(range(NEAR)))
    hits = jnp.concatenate(
        [
            one_hot(jnp.where(quad == distance * members + half, slot, -1), size)
            for distance in order
            for half in range(members)
        ],
        axis=0,
    )
    all_both = dot(hits, pieces)
    for step, distance in enumerate(order):
        for half in range(members):
            at = distance * members + half
            extra = jnp.zeros((rows, LANES), jnp.float32)
            for i in range(2 * parts):
                label = labels[i * quads + at : i * quads + at + 1]
                extra = jnp.where(row_id == capacity + i, label, extra)
            place = step * members + half
            both = all_both[place * size : (place + 1) * size]
            picked = both[:, :LANES] + both[:, LANES:]
            for q in range(F):
                message = extra
                for g in range(GROUPS):
                    shift = (KW * (g - (field ^ q))) & (LANES - 1)
                    turned = pltpu.roll(picked[g * rows : (g + 1) * rows], shift, 1)
                    message = jnp.where((lane_group == g) & (row_id < capacity), turned, message)
                if distance < NEAR:
                    near[distance][q, half] = message
                else:
                    far[q][distance - NEAR, half] = message


def prepare_kernel(members, lon_cols, zonal, vert, zonal_high, zonal_low, vert_both, turned):
    position = lax.axis_index("lon")
    f, h = position // members, lax.rem(position, members)
    turned[...] = zonal[...].T
    for e in range(members):
        for q in range(F):
            block = (f ^ q) * members + lax.rem(h + e, members)
            part = turned[pl.ds(pl.multiple_of(block * lon_cols, lon_cols), lon_cols), :]
            at = slice((e * F + q) * lon_cols, (e * F + q + 1) * lon_cols)
            zonal_high[at], zonal_low[at] = split(part)
    high, low = split(vert[f])
    vert_both[:LEV, :LEV] = high
    vert_both[:LEV, LEV:] = low
    vert_both[LEV:, :LEV] = high
    vert_both[LEV:, LEV:] = jnp.zeros_like(low)


def scatter(pieces, half, capacity, columns):
    rows = pieces[0].shape[0]
    count = len(pieces)
    slots = -(-count * rows // LANES) * LANES
    parts, _ = message_rows(capacity)
    row_id, lane_id = iota((rows, LANES), 0), iota((rows, LANES), 1)
    piece_id = row_id >> (KW.bit_length() - 1)
    diagonal = ((lane_id & (KW - 1)) == (row_id & (KW - 1))) & (row_id < capacity)
    empty = jnp.where((row_id >= capacity) & ((lane_id & (KW - 1)) == 0), -1.0, 0.0)
    cells, offsets = [], []
    for piece in pieces:
        cell, offset = empty, jnp.zeros((rows, LANES), jnp.float32)
        for p in range(parts):
            mine = diagonal & (piece_id == p)
            at = capacity + 2 * p
            cell = jnp.where(mine, piece[at : at + 1], cell)
            offset = jnp.where(mine, piece[at + 1 : at + 2], offset)
        cells.append(cell)
        offsets.append(offset)
    spare = slots - count * rows
    if spare:
        pieces = pieces + [jnp.zeros((spare, LANES), jnp.float32)]
        cells.append(jnp.full((spare, LANES), -1.0, jnp.float32))
        offsets.append(jnp.zeros((spare, LANES), jnp.float32))
    values = jnp.concatenate(pieces, axis=0)
    cells = jnp.concatenate(cells, axis=0).astype(jnp.bfloat16)
    offsets = jnp.concatenate(offsets, axis=0).astype(jnp.bfloat16)
    wide = (LANES, GROUPS * LEV)
    spread = (
        iota(wide, 0) >> (KW.bit_length() - 1) == iota(wide, 1) >> (LEV.bit_length() - 1)
    ).astype(jnp.bfloat16)
    picker = (
        iota((SUBLANES, LANES), 0) == iota((SUBLANES, LANES), 1) >> (KW.bit_length() - 1)
    ).astype(jnp.bfloat16)
    cell_rows = lax.dot_general(
        picker, cells, (((1,), (1,)), ((), ())), preferred_element_type=jnp.float32
    )
    middle = iota((slots, LEV), 1).astype(jnp.float32) - (KW - 1) / 2
    sums = []
    for g in range(GROUPS):
        if g % 2 == 0:
            starts = dot(offsets, spread[:, g * LEV : (g + 2) * LEV])
        inside = jnp.abs(middle - starts[:, (g % 2) * LEV : (g % 2 + 1) * LEV]) < KW / 2
        source = g * KW + (iota((slots, LANES), 1) & (KW - 1))
        tiled = jnp.take_along_axis(values, source, axis=1, mode="promise_in_bounds")
        placed = jnp.concatenate(split(jnp.where(inside, tiled, 0.0)), axis=1)
        both = dot(one_hot(cell_rows[g : g + 1], columns), placed)
        sums.append(both[:, :LEV] + both[:, LEV:])
    return sums


def early_kernel(capacity, *refs):
    received, out = refs[:-1], refs[-1]
    halves, columns = received[0].shape[1], out.shape[1]
    for half in range(halves):
        pieces = [ref[k, half] for ref in received for k in range(ref.shape[0])]
        for g, total in enumerate(scatter(pieces, half, capacity, columns)):
            out[half * GROUPS + g] = total


def late_kernel(capacity, lon_cols, count, *refs):
    received = refs[:count]
    early, zonal_high, zonal_low, vert_both, high_out, low_out, *partials = refs[count:]
    halves, columns = received[0].shape[1], early.shape[1]
    for half in range(halves):
        pieces = [ref[k, half] for ref in received for k in range(ref.shape[0])]
        for g, total in enumerate(scatter(pieces, half, capacity, columns)):
            block = half * GROUPS + g
            adjoint_high, adjoint_low = split(early[block] + total)
            both = dot(jnp.concatenate([adjoint_high, adjoint_low], axis=1), vert_both[...])
            vertical = both[:, :LEV] + both[:, LEV:]
            high, low = split(vertical)
            for a in range(columns // lon_cols):
                at = slice(block * lon_cols, (block + 1) * lon_cols)
                rows = slice(a * lon_cols, (a + 1) * lon_cols)
                high_out[at, a * LEV : (a + 1) * LEV] = high[rows]
                low_out[at, a * LEV : (a + 1) * LEV] = low[rows]
    for e, partial in enumerate(partials, 1):
        partial[...] = zonal_product(e, zonal_high, zonal_low, high_out, low_out, partial.shape[0])


def zonal_product(e, zonal_high, zonal_low, high, low, size):
    at = slice(e * size, (e + 1) * size)
    first = dot(zonal_high[at], high[...]) + dot(zonal_low[at], high[...])
    return first + dot(zonal_high[at], low[...])


def own_kernel(zonal_high, zonal_low, high, low, out):
    out[...] = zonal_product(0, zonal_high, zonal_low, high, low, out.shape[0])


def sum_kernel(lon_cols, *refs):
    terms, outs = refs[:-F], refs[-F:]
    for q in range(F):
        at = slice(q * lon_cols, (q + 1) * lon_cols)
        total = terms[0][at]
        for term in terms[1:]:
            total = total + term[at]
        outs[q][...] = total


def finish_kernel(members, control, *refs):
    parts, out = refs[:F], refs[F]
    field = lax.axis_index("lon") // members
    for q in range(F):
        at = pl.ds(pl.multiple_of((field ^ q) * LEV, LEV), LEV)
        for a in range(control.shape[0]):
            out[a, :, at] = control[a, :, at] + parts[q][:, a * LEV : (a + 1) * LEV]


def call(kernel, out_shape, n_in, vmem=24, flops=0, nbytes=0, scratch=()):
    one = pl.BlockSpec(memory_space=pltpu.VMEM)
    return pl.pallas_call(
        kernel,
        out_shape=out_shape,
        in_specs=[one] * n_in,
        out_specs=[one] * len(out_shape) if isinstance(out_shape, (list, tuple)) else one,
        scratch_shapes=list(scratch),
        compiler_params=pltpu.CompilerParams(vmem_limit_bytes=vmem * MIB),
        cost_estimate=pl.CostEstimate(flops=flops, bytes_accessed=nbytes, transcendentals=0),
    )


def along_lat(x, d):
    lats = lax.axis_size("lat")
    return lax.ppermute(x, "lat", [(i, i ^ d ^ ((i & d & 2) >> 1)) for i in range(lats)])


def to_field(x, q, members):
    if q == 0:
        return x
    lons = lax.axis_size("lon")
    return lax.ppermute(
        x, "lon", [(i, (i // members ^ q) * members + i % members) for i in range(lons)]
    )


def to_member(x, e, members):
    lons = lax.axis_size("lon")
    return lax.ppermute(
        x, "lon", [(i, i // members * members + (i + e) % members) for i in range(lons)]
    )


def per_device(
    control,
    vert_factor,
    zonal_factor,
    obs_dest,
    obs_cell,
    obs_offset,
    obs_count,
    departure,
    obs_rinv,
    obs_weights,
):
    lats = lax.axis_size("lat")
    lons = lax.axis_size("lon")
    devices = lats * lons
    members = lons // F
    n_obs = obs_cell.shape[0]
    capacity = max(2, 3 * n_obs // (2 * devices))
    _, rows = message_rows(capacity)
    lat_rows, lon_cols, _ = control.shape
    columns = lat_rows * lon_cols
    blocks = lons
    all_lons = lons * lon_cols
    share = F * lon_cols
    wide = lat_rows * LEV
    f32, bf16 = jnp.float32, jnp.bfloat16
    far_messages = jax.ShapeDtypeStruct((lats - NEAR, members, rows, LANES), f32)
    near_messages = jax.ShapeDtypeStruct((F, members, rows, LANES), f32)
    messages = pl.pallas_call(
        functools.partial(pack_kernel, members, capacity, lats),
        out_shape=[far_messages] * F + [near_messages] * NEAR,
        in_specs=[pl.BlockSpec(memory_space=pltpu.HBM)] * 7,
        out_specs=[pl.BlockSpec(memory_space=pltpu.VMEM)] * (F + NEAR),
        scratch_shapes=[
            pltpu.SMEM((1, 1), jnp.int32),
            pltpu.VMEM((1, n_obs), jnp.int32),
            pltpu.VMEM((n_obs,), jnp.int32),
            pltpu.VMEM((n_obs,), jnp.int32),
            pltpu.VMEM((n_obs,), f32),
            pltpu.VMEM((n_obs,), f32),
            pltpu.VMEM((n_obs, LANES), f32),
            pltpu.SemaphoreType.DMA((7,)),
        ],
        compiler_params=pltpu.CompilerParams(vmem_limit_bytes=24 * MIB),
        cost_estimate=pl.CostEstimate(
            flops=4 * devices * rows * n_obs * LANES, bytes_accessed=1 << 20, transcendentals=0
        ),
    )(
        obs_count.reshape(1, 1),
        *(
            pltpu.with_memory_space_constraint(x, pltpu.HBM)
            for x in (
                obs_dest.reshape(1, n_obs),
                obs_cell,
                obs_offset,
                departure,
                obs_rinv,
                obs_weights,
            )
        )
    )
    far = [to_field(messages[q], q, members) for q in range(F)]
    late = [
        along_lat(jnp.stack([part[d - NEAR] for part in far]), d)
        for d in reversed(range(NEAR, lats))
    ]
    near = [messages[F]] + [along_lat(messages[F + d], d) for d in range(1, NEAR)]
    near = [to_field(jnp.stack([part[q] for part in near]), q, members) for q in range(F)]
    zonal_high, zonal_low, vert_both = call(
        functools.partial(prepare_kernel, members, lon_cols),
        [
            jax.ShapeDtypeStruct((members * share, all_lons), bf16),
            jax.ShapeDtypeStruct((members * share, all_lons), bf16),
            jax.ShapeDtypeStruct((2 * LEV, 2 * LEV), bf16),
        ],
        2,
        scratch=[pltpu.VMEM(zonal_factor.shape, f32)],
        nbytes=2 << 20,
    )(zonal_factor, vert_factor)
    early = call(
        functools.partial(early_kernel, capacity),
        jax.ShapeDtypeStruct((blocks, columns, LEV), f32),
        F,
        vmem=24,
        flops=4 * blocks * columns * NEAR * F * rows * LEV,
        nbytes=2 << 20,
    )(*near)
    partial = jax.ShapeDtypeStruct((share, wide), f32)
    half_vertical = jax.ShapeDtypeStruct((all_lons, wide), bf16)
    high, low, *partials = call(
        functools.partial(late_kernel, capacity, lon_cols, len(late)),
        [half_vertical] * 2 + [partial] * (members - 1),
        4 + len(late),
        vmem=24,
        flops=6 * members * share * all_lons * wide,
        nbytes=2 << 20,
    )(*late, early, zonal_high, zonal_low, vert_both)
    others = [to_member(partials[e - 1], e, members) for e in range(1, members)]
    own = call(
        own_kernel, partial, 4, flops=6 * share * all_lons * wide, nbytes=1 << 20
    )(zonal_high, zonal_low, high, low)
    products = call(
        functools.partial(sum_kernel, lon_cols),
        [jax.ShapeDtypeStruct((lon_cols, wide), f32)] * F,
        members,
        nbytes=1 << 20,
    )(own, *others)
    parts = [to_field(products[q], q, members) for q in range(F)]
    return call(
        functools.partial(finish_kernel, members),
        jax.ShapeDtypeStruct(control.shape, f32),
        1 + F,
        nbytes=2 << 20,
    )(control, *parts)


def solution(mesh):
    return jax.shard_map(
        per_device,
        mesh=mesh,
        in_specs=(
            P("lat", "lon", None),
            P(),
            P(),
            P(("lat", "lon"), None),
            P(("lat", "lon")),
            P(("lat", "lon")),
            P(("lat", "lon")),
            P(("lat", "lon")),
            P(("lat", "lon")),
            P(("lat", "lon"), None),
        ),
        out_specs=P("lat", "lon", None),
        check_vma=False,
    )
```

```python
import functools

import jax
import jax.numpy as jnp
from jax import lax
from jax.experimental import pallas as pl
from jax.experimental.pallas import tpu as pltpu
from jax.sharding import PartitionSpec as P

F = 4
LEV = 128
KW = 32
LANES = 128
SUBLANES = 8
GROUPS = LANES // KW
NEAR = 2
MIB = 1 << 20


def iota(shape, axis):
    return lax.broadcasted_iota(jnp.int32, shape, axis)


def split(x):
    high = x.astype(jnp.bfloat16)
    return high, (x - high.astype(jnp.float32)).astype(jnp.bfloat16)


def dot(a, b):
    return jnp.dot(a, b, preferred_element_type=jnp.float32)


def one_hot(labels, size):
    hit = iota((size, labels.shape[1]), 0).astype(jnp.bfloat16) == labels.astype(jnp.bfloat16)
    return jnp.where(hit, jnp.bfloat16(1), jnp.bfloat16(0))


def message_rows(capacity):
    parts = -(-capacity // KW)
    return parts, -(-(capacity + 2 * parts) // SUBLANES) * SUBLANES


def pack_kernel(members, capacity, lats, *refs):
    sources, far, near = refs[:7], refs[7 : 7 + F], refs[7 + F : 7 + F + NEAR]
    held, by_field, arrived = refs[7 + F + NEAR : -2], refs[-2], refs[-1]
    loads = [
        pltpu.make_async_copy(source, target, arrived.at[i])
        for i, (source, target) in enumerate(zip(sources, held))
    ]
    for load in loads:
        load.start()
    count, dest, cell, offset, departure, rinv, weights = held
    n = weights.shape[0]
    rows = far[0].shape[2]
    lons = F * members
    devices = lats * lons
    field = lax.axis_index("lon") // members
    parts, _ = message_rows(capacity)
    quads = devices // GROUPS
    chunks = n // LANES
    loads[1].wait()
    lat = lax.axis_index("lat")
    band = dest[...] // lons ^ lat
    dest_row = (band ^ ((band & lat & 2) >> 1)) * lons + lax.rem(dest[...], lons)
    hits = [
        iota((devices, LANES), 0) == dest_row[:, c * LANES : (c + 1) * LANES] for c in range(chunks)
    ]
    stacked = jnp.concatenate([hit.astype(jnp.bfloat16) for hit in hits], axis=0)
    before = (iota((LANES, 2 * LANES), 0) < iota((LANES, 2 * LANES), 1)).astype(jnp.bfloat16)
    counts = dot(stacked, before)
    carry = jnp.zeros((devices, LANES), jnp.float32)
    ranks = []
    for c in range(chunks):
        part = counts[c * devices : (c + 1) * devices]
        ranks.append(
            jnp.sum(jnp.where(hits[c], part[:, :LANES] + carry, 0.0), axis=0, keepdims=True)
        )
        carry = carry + part[:, LANES:]
    rank = jnp.concatenate(ranks, axis=1).astype(jnp.int32)
    group = dest_row & (GROUPS - 1)
    quad = dest_row >> (GROUPS.bit_length() - 1)
    slot = group * rows + rank
    lane = group * KW + (rank & (KW - 1))
    piece = rank >> (KW.bit_length() - 1)
    for i in (0, 2, 3, 4, 5):
        loads[i].wait()
    cell_row, offset_row = cell[...].reshape(1, n), offset[...].reshape(1, n)
    live = iota((1, n), 1) < count[0, 0]
    scaled = jnp.where(
        live, rinv[...].reshape(1, n) * departure[...].reshape(1, n), jnp.float32(0.0)
    )
    columns = jnp.concatenate(
        [
            scaled,
            lane.astype(jnp.float32),
            offset_row.astype(jnp.float32),
            jnp.zeros((SUBLANES - 3, n), jnp.float32),
        ],
        axis=0,
    ).T
    lane_id = iota((n, LANES), 1)
    lane_hit = (columns[:, 1:2].astype(jnp.int32) == lane_id).astype(jnp.bfloat16)
    label_rows = []
    for p in range(parts):
        for label in (cell_row, offset_row):
            mine = (iota((quads, n), 0) == quad) & (piece == p)
            label_rows.append(jnp.where(mine, label.astype(jnp.float32), 0.0))
    labels = dot(jnp.concatenate(label_rows, axis=0).astype(jnp.bfloat16), lane_hit)
    source = (lane_id & -KW) | ((lane_id - columns[:, 2:3].astype(jnp.int32)) & (KW - 1))
    loads[6].wait()
    turned = jnp.take_along_axis(weights[...], source, axis=1, mode="promise_in_bounds")
    high, low = split(turned * columns[:, 0:1])
    pieces = jnp.concatenate([high, low], axis=1)
    even = iota((rows, LANES), 1) & KW == 0
    lower = iota((rows, LANES), 1) < LANES // 2
    size = GROUPS * rows
    tail = capacity // SUBLANES * SUBLANES
    row_id = iota((rows - tail, LANES), 0) + tail
    order = (*range(NEAR, lats), *reversed(range(NEAR)))
    hits = jnp.concatenate(
        [
            one_hot(jnp.where(quad == distance * members + half, slot, -1), size)
            for distance in order
            for half in range(members)
        ],
        axis=0,
    )
    both = dot(hits, pieces)
    for step, distance in enumerate(order):
        for half in range(members):
            at = (step * members + half) * size
            picked = both[at : at + size, :LANES] + both[at : at + size, LANES:]
            blocks = [picked[g * rows : (g + 1) * rows] for g in range(GROUPS)]
            pairs = [
                part
                for i in (0, 2)
                for part in (
                    jnp.where(even, blocks[i], pltpu.roll(blocks[i + 1], KW, 1)),
                    jnp.where(even, pltpu.roll(blocks[i], LANES - KW, 1), blocks[i + 1]),
                )
            ]
            fields = [
                jnp.where(lower, pairs[0], pltpu.roll(pairs[2], LANES // 2, 1)),
                jnp.where(lower, pairs[1], pltpu.roll(pairs[3], LANES // 2, 1)),
                jnp.where(lower, pltpu.roll(pairs[0], LANES // 2, 1), pairs[2]),
                jnp.where(lower, pltpu.roll(pairs[1], LANES // 2, 1), pairs[3]),
            ]
            extra = jnp.zeros((rows - tail, LANES), jnp.float32)
            for i in range(2 * parts):
                k = i * quads + distance * members + half
                extra = jnp.where(row_id == capacity + i, labels[k : k + 1], extra)
            for f in range(F):
                message = jnp.concatenate([fields[f][:tail], fields[f][tail:] + extra], axis=0)
                if distance < NEAR:
                    near[distance][field ^ f, half] = message
                else:
                    by_field[distance - NEAR, half, f] = message
            if distance >= NEAR:
                for q in range(F):
                    far[q][distance - NEAR, half] = by_field[distance - NEAR, half, field ^ q]


def prepare_kernel(members, lon_cols, zonal, vert, zonal_high, zonal_low, vert_both, turned):
    position = lax.axis_index("lon")
    f, h = position // members, lax.rem(position, members)
    turned[...] = zonal[...].T
    for e in range(members):
        for q in range(F):
            block = (f ^ q) * members + lax.rem(h + e, members)
            part = turned[pl.ds(pl.multiple_of(block * lon_cols, lon_cols), lon_cols), :]
            at = slice((e * F + q) * lon_cols, (e * F + q + 1) * lon_cols)
            zonal_high[at], zonal_low[at] = split(part)
    high, low = split(vert[f])
    vert_both[:LEV, :LEV] = high
    vert_both[:LEV, LEV:] = low
    vert_both[LEV:, :LEV] = high
    vert_both[LEV:, LEV:] = jnp.zeros_like(low)


def scatter(pieces, half, capacity, columns):
    rows = pieces[0].shape[0]
    count = len(pieces)
    slots = -(-count * rows // LANES) * LANES
    parts, _ = message_rows(capacity)
    row_id, lane_id = iota((rows, LANES), 0), iota((rows, LANES), 1)
    piece_id = row_id >> (KW.bit_length() - 1)
    diagonal = ((lane_id & (KW - 1)) == (row_id & (KW - 1))) & (row_id < capacity)
    empty = jnp.where((row_id >= capacity) & ((lane_id & (KW - 1)) == 0), -1.0, 0.0)
    labels = []
    for piece in pieces:
        cell, offset = empty, jnp.zeros((rows, LANES), jnp.float32)
        for p in range(parts):
            mine = diagonal & (piece_id == p)
            at = capacity + 2 * p
            cell = jnp.where(mine, piece[at : at + 1], cell)
            offset = jnp.where(mine, piece[at + 1 : at + 2], offset)
        labels.append(jnp.concatenate([cell, offset], axis=1))
    spare = slots - count * rows
    if spare:
        pieces = pieces + [jnp.zeros((spare, LANES), jnp.float32)]
        labels.append(jnp.full((spare, 2 * LANES), -1.0, jnp.float32))
    picker = (
        iota((2 * GROUPS, 2 * LANES), 0) == iota((2 * GROUPS, 2 * LANES), 1) >> (KW.bit_length() - 1)
    ).astype(jnp.bfloat16)
    along = (((1,), (1,)), ((), ()))
    label_rows = lax.dot_general(
        picker,
        jnp.concatenate(labels, axis=0).astype(jnp.bfloat16),
        along,
        preferred_element_type=jnp.float32,
    ).astype(jnp.bfloat16)
    high, low = split(jnp.concatenate(pieces, axis=0).T)
    middle = iota((LEV, slots), 0).astype(jnp.bfloat16) - jnp.bfloat16((KW - 1) / 2)
    sums = []
    for g in range(GROUPS):
        at = slice(g * KW, (g + 1) * KW)
        inside = jnp.abs(middle - label_rows[GROUPS + g : GROUPS + g + 1]) < jnp.bfloat16(KW / 2)
        placed = jnp.concatenate(
            [
                jnp.where(inside, jnp.concatenate([piece[at]] * (LEV // KW), axis=0), jnp.bfloat16(0))
                for piece in (high, low)
            ],
            axis=0,
        )
        both = lax.dot_general(
            one_hot(label_rows[g : g + 1], columns),
            placed,
            along,
            preferred_element_type=jnp.float32,
        )
        sums.append(both[:, :LEV] + both[:, LEV:])
    return sums


def early_kernel(capacity, *refs):
    received, out = refs[:-1], refs[-1]
    halves, columns = received[0].shape[1], out.shape[1]
    for half in range(halves):
        pieces = [ref[k, half] for ref in received for k in range(ref.shape[0])]
        for g, total in enumerate(scatter(pieces, half, capacity, columns)):
            out[half * GROUPS + g] = total


def late_kernel(capacity, lon_cols, count, *refs):
    received = refs[:count]
    early, zonal_high, zonal_low, vert_both, high_out, low_out, *partials = refs[count:]
    halves, columns = received[0].shape[1], early.shape[1]
    for half in range(halves):
        pieces = [ref[k, half] for ref in received for k in range(ref.shape[0])]
        for g, total in enumerate(scatter(pieces, half, capacity, columns)):
            block = half * GROUPS + g
            adjoint_high, adjoint_low = split(early[block] + total)
            both = dot(jnp.concatenate([adjoint_high, adjoint_low], axis=1), vert_both[...])
            vertical = both[:, :LEV] + both[:, LEV:]
            high, low = split(vertical)
            for a in range(columns // lon_cols):
                at = slice(block * lon_cols, (block + 1) * lon_cols)
                rows = slice(a * lon_cols, (a + 1) * lon_cols)
                high_out[at, a * LEV : (a + 1) * LEV] = high[rows]
                low_out[at, a * LEV : (a + 1) * LEV] = low[rows]
    for e, partial in enumerate(partials, 1):
        partial[...] = zonal_product(e, zonal_high, zonal_low, high_out, low_out, partial.shape[0])


def zonal_product(e, zonal_high, zonal_low, high, low, size):
    at = slice(e * size, (e + 1) * size)
    first = dot(zonal_high[at], high[...]) + dot(zonal_low[at], high[...])
    return first + dot(zonal_high[at], low[...])


def own_kernel(zonal_high, zonal_low, high, low, out):
    out[...] = zonal_product(0, zonal_high, zonal_low, high, low, out.shape[0])


def sum_kernel(lon_cols, *refs):
    terms, outs = refs[:-F], refs[-F:]
    for q in range(F):
        at = slice(q * lon_cols, (q + 1) * lon_cols)
        total = terms[0][at]
        for term in terms[1:]:
            total = total + term[at]
        outs[q][...] = total


def finish_kernel(members, distances, *refs):
    count = len(distances)
    control, parts = refs[0], refs[1 : 1 + count]
    out, held, sent = refs[-3:]
    field = lax.axis_index("lon") // members
    copies = []
    for i, q in enumerate(distances):
        at = pl.ds(pl.multiple_of((field ^ q) * LEV, LEV), LEV)
        for a in range(control.shape[0]):
            held[i, a] = control[a, :, at] + parts[i][:, a * LEV : (a + 1) * LEV]
        copies.append(pltpu.make_async_copy(held.at[i], out.at[:, :, at], sent.at[i]))
        copies[-1].start()
    for copy in copies:
        copy.wait()


def call(kernel, out_shape, n_in, vmem=24, flops=0, nbytes=0, scratch=()):
    one = pl.BlockSpec(memory_space=pltpu.VMEM)
    return pl.pallas_call(
        kernel,
        out_shape=out_shape,
        in_specs=[one] * n_in,
        out_specs=[one] * len(out_shape) if isinstance(out_shape, (list, tuple)) else one,
        scratch_shapes=list(scratch),
        compiler_params=pltpu.CompilerParams(vmem_limit_bytes=vmem * MIB),
        cost_estimate=pl.CostEstimate(flops=flops, bytes_accessed=nbytes, transcendentals=0),
    )


def along_lat(x, d):
    lats = lax.axis_size("lat")
    return lax.ppermute(x, "lat", [(i, i ^ d ^ ((i & d & 2) >> 1)) for i in range(lats)])


def to_field(x, q, members):
    if q == 0:
        return x
    lons = lax.axis_size("lon")
    return lax.ppermute(
        x, "lon", [(i, (i // members ^ q) * members + i % members) for i in range(lons)]
    )


def to_member(x, e, members):
    lons = lax.axis_size("lon")
    return lax.ppermute(
        x, "lon", [(i, i // members * members + (i + e) % members) for i in range(lons)]
    )


def per_device(
    control,
    vert_factor,
    zonal_factor,
    obs_dest,
    obs_cell,
    obs_offset,
    obs_count,
    departure,
    obs_rinv,
    obs_weights,
):
    lats = lax.axis_size("lat")
    lons = lax.axis_size("lon")
    devices = lats * lons
    members = lons // F
    n_obs = obs_cell.shape[0]
    capacity = max(2, 3 * n_obs // (2 * devices))
    _, rows = message_rows(capacity)
    lat_rows, lon_cols, _ = control.shape
    columns = lat_rows * lon_cols
    blocks = lons
    all_lons = lons * lon_cols
    share = F * lon_cols
    wide = lat_rows * LEV
    f32, bf16 = jnp.float32, jnp.bfloat16
    far_messages = jax.ShapeDtypeStruct((lats - NEAR, members, rows, LANES), f32)
    near_messages = jax.ShapeDtypeStruct((F, members, rows, LANES), f32)
    messages = pl.pallas_call(
        functools.partial(pack_kernel, members, capacity, lats),
        out_shape=[far_messages] * F + [near_messages] * NEAR,
        in_specs=[pl.BlockSpec(memory_space=pltpu.HBM)] * 7,
        out_specs=[pl.BlockSpec(memory_space=pltpu.VMEM)] * (F + NEAR),
        scratch_shapes=[
            pltpu.SMEM((1, 1), jnp.int32),
            pltpu.VMEM((1, n_obs), jnp.int32),
            pltpu.VMEM((n_obs,), jnp.int32),
            pltpu.VMEM((n_obs,), jnp.int32),
            pltpu.VMEM((n_obs,), f32),
            pltpu.VMEM((n_obs,), f32),
            pltpu.VMEM((n_obs, LANES), f32),
            pltpu.VMEM((lats - NEAR, members, F, rows, LANES), f32),
            pltpu.SemaphoreType.DMA((7,)),
        ],
        compiler_params=pltpu.CompilerParams(vmem_limit_bytes=24 * MIB),
        cost_estimate=pl.CostEstimate(
            flops=4 * devices * rows * n_obs * LANES, bytes_accessed=1 << 20, transcendentals=0
        ),
    )(
        obs_count.reshape(1, 1),
        *(
            pltpu.with_memory_space_constraint(x, pltpu.HBM)
            for x in (
                obs_dest.reshape(1, n_obs),
                obs_cell,
                obs_offset,
                departure,
                obs_rinv,
                obs_weights,
            )
        )
    )
    far, near = list(messages[:F]), list(messages[F:])
    far = [to_field(far[q], q, members) for q in range(F)]
    late = [
        along_lat(jnp.stack([part[d - NEAR] for part in far]), d)
        for d in reversed(range(NEAR, lats))
    ]
    near = near[:1] + [along_lat(near[d], d) for d in range(1, NEAR)]
    near = [to_field(jnp.stack([part[q] for part in near]), q, members) for q in range(F)]
    zonal_high, zonal_low, vert_both = call(
        functools.partial(prepare_kernel, members, lon_cols),
        [
            jax.ShapeDtypeStruct((members * share, all_lons), bf16),
            jax.ShapeDtypeStruct((members * share, all_lons), bf16),
            jax.ShapeDtypeStruct((2 * LEV, 2 * LEV), bf16),
        ],
        2,
        scratch=[pltpu.VMEM(zonal_factor.shape, f32)],
        nbytes=2 << 20,
    )(zonal_factor, vert_factor)
    early = call(
        functools.partial(early_kernel, capacity),
        jax.ShapeDtypeStruct((blocks, columns, LEV), f32),
        F,
        vmem=24,
        flops=4 * blocks * columns * NEAR * F * rows * LEV,
        nbytes=2 << 20,
    )(*near)
    partial = jax.ShapeDtypeStruct((share, wide), f32)
    half_vertical = jax.ShapeDtypeStruct((all_lons, wide), bf16)
    high, low, *partials = call(
        functools.partial(late_kernel, capacity, lon_cols, len(late)),
        [half_vertical] * 2 + [partial] * (members - 1),
        4 + len(late),
        vmem=24,
        flops=6 * members * share * all_lons * wide,
        nbytes=2 << 20,
    )(*late, early, zonal_high, zonal_low, vert_both)
    others = [to_member(partials[e - 1], e, members) for e in range(1, members)]
    own = call(
        own_kernel, partial, 4, flops=6 * share * all_lons * wide, nbytes=1 << 20
    )(zonal_high, zonal_low, high, low)
    products = call(
        functools.partial(sum_kernel, lon_cols),
        [jax.ShapeDtypeStruct((lon_cols, wide), f32)] * F,
        members,
        nbytes=1 << 20,
    )(own, *others)
    parts = [to_field(products[q], q, members) for q in range(F)]
    out = ()
    for distances in ((0, 1), (2, 3)):
        count = len(distances)
        out = (
            pl.pallas_call(
                functools.partial(finish_kernel, members, distances),
                out_shape=jax.ShapeDtypeStruct(control.shape, f32),
                in_specs=[pl.BlockSpec(memory_space=pltpu.VMEM)] * (1 + count)
                + [pl.BlockSpec(memory_space=pltpu.HBM)] * len(out),
                out_specs=pl.BlockSpec(memory_space=pltpu.HBM),
                scratch_shapes=[
                    pltpu.VMEM((count, lat_rows, lon_cols, LEV), f32),
                    pltpu.SemaphoreType.DMA((count,)),
                ],
                input_output_aliases={1 + count: 0} if out else {},
                compiler_params=pltpu.CompilerParams(vmem_limit_bytes=24 * MIB),
                cost_estimate=pl.CostEstimate(
                    flops=0, bytes_accessed=count << 19, transcendentals=0
                ),
            )(control, *(parts[q] for q in distances), *out),
        )
    return out[0]


def solution(mesh):
    return jax.shard_map(
        per_device,
        mesh=mesh,
        in_specs=(
            P("lat", "lon", None),
            P(),
            P(),
            P(("lat", "lon"), None),
            P(("lat", "lon")),
            P(("lat", "lon")),
            P(("lat", "lon")),
            P(("lat", "lon")),
            P(("lat", "lon")),
            P(("lat", "lon"), None),
        ),
        out_specs=P("lat", "lon", None),
        check_vma=False,
    )
```

```python
import functools

import jax
import jax.numpy as jnp
from jax import lax
from jax.experimental import pallas as pl
from jax.experimental.pallas import tpu as pltpu
from jax.sharding import PartitionSpec as P

F = 4
LEV = 128
KW = 32
LANES = 128
SUBLANES = 8
GROUPS = LANES // KW
NEAR = 2
MIB = 1 << 20


def iota(shape, axis):
    return lax.broadcasted_iota(jnp.int32, shape, axis)


def split(x):
    high = x.astype(jnp.bfloat16)
    return high, (x - high.astype(jnp.float32)).astype(jnp.bfloat16)


def dot(a, b):
    return jnp.dot(a, b, preferred_element_type=jnp.float32)


def one_hot(labels, size):
    hit = iota((size, labels.shape[1]), 0).astype(jnp.bfloat16) == labels.astype(jnp.bfloat16)
    return jnp.where(hit, jnp.bfloat16(1), jnp.bfloat16(0))


def message_rows(capacity):
    parts = -(-capacity // KW)
    return parts, -(-(capacity + 2 * parts) // SUBLANES) * SUBLANES


def pack_kernel(members, capacity, lats, *refs):
    sources, far, near = refs[:7], refs[7 : 7 + F], refs[7 + F : 7 + F + NEAR]
    held, by_field, arrived = refs[7 + F + NEAR : -2], refs[-2], refs[-1]
    loads = [
        pltpu.make_async_copy(source, target, arrived.at[i])
        for i, (source, target) in enumerate(zip(sources, held))
    ]
    for i in (1, 6, 0, 2, 3, 4, 5):
        loads[i].start()
    count, dest, cell, offset, departure, rinv, weights = held
    n = weights.shape[0]
    rows = far[0].shape[2]
    lons = F * members
    devices = lats * lons
    field = lax.axis_index("lon") // members
    parts, _ = message_rows(capacity)
    quads = devices // GROUPS
    chunks = n // LANES
    loads[1].wait()
    lat = lax.axis_index("lat")
    band = dest[...] // lons ^ lat
    dest_row = (band ^ ((band & lat & 2) >> 1)) * lons + lax.rem(dest[...], lons)
    hits = [
        iota((devices, LANES), 0) == dest_row[:, c * LANES : (c + 1) * LANES] for c in range(chunks)
    ]
    stacked = jnp.concatenate([hit.astype(jnp.bfloat16) for hit in hits], axis=0)
    before = (iota((LANES, 2 * LANES), 0) < iota((LANES, 2 * LANES), 1)).astype(jnp.bfloat16)
    counts = dot(stacked, before)
    carry = jnp.zeros((devices, LANES), jnp.float32)
    ranks = []
    for c in range(chunks):
        part = counts[c * devices : (c + 1) * devices]
        ranks.append(
            jnp.sum(jnp.where(hits[c], part[:, :LANES] + carry, 0.0), axis=0, keepdims=True)
        )
        carry = carry + part[:, LANES:]
    rank = jnp.concatenate(ranks, axis=1).astype(jnp.int32)
    group = dest_row & (GROUPS - 1)
    quad = dest_row >> (GROUPS.bit_length() - 1)
    slot = group * rows + rank
    lane = group * KW + (rank & (KW - 1))
    piece = rank >> (KW.bit_length() - 1)
    for i in (0, 2, 3, 4, 5):
        loads[i].wait()
    cell_row, offset_row = cell[...].reshape(1, n), offset[...].reshape(1, n)
    live = iota((1, n), 1) < count[0, 0]
    scaled = jnp.where(
        live, rinv[...].reshape(1, n) * departure[...].reshape(1, n), jnp.float32(0.0)
    )
    columns = jnp.concatenate(
        [scaled, offset_row.astype(jnp.float32), jnp.zeros((SUBLANES - 2, n), jnp.float32)], axis=0
    ).T
    lane_id = iota((n, LANES), 1)
    label_rows = []
    for p in range(parts):
        for label in (cell_row, offset_row):
            mine = (iota((quads, n), 0) == quad) & (piece == p)
            label_rows.append(jnp.where(mine, label.astype(jnp.float32), 0.0))
    labels = lax.dot_general(
        jnp.concatenate(label_rows, axis=0).astype(jnp.bfloat16),
        one_hot(lane, LANES),
        (((1,), (1,)), ((), ())),
        preferred_element_type=jnp.float32,
    )
    source = (lane_id & -KW) | ((lane_id - columns[:, 1:2].astype(jnp.int32)) & (KW - 1))
    loads[6].wait()
    turned = jnp.take_along_axis(weights[...], source, axis=1, mode="promise_in_bounds")
    high, low = split(turned * columns[:, 0:1])
    pieces = jnp.concatenate([high, low], axis=1)
    even = iota((rows, LANES), 1) & KW == 0
    lower = iota((rows, LANES), 1) < LANES // 2
    size = GROUPS * rows
    tail = capacity // SUBLANES * SUBLANES
    row_id = iota((rows - tail, LANES), 0) + tail
    order = (*range(NEAR, lats), *reversed(range(NEAR)))
    hits = jnp.concatenate(
        [
            one_hot(jnp.where(quad == distance * members + half, slot, -1), size)
            for distance in order
            for half in range(members)
        ],
        axis=0,
    )
    both = dot(hits, pieces)
    for step, distance in enumerate(order):
        for half in range(members):
            at = (step * members + half) * size
            picked = both[at : at + size, :LANES] + both[at : at + size, LANES:]
            blocks = [picked[g * rows : (g + 1) * rows] for g in range(GROUPS)]
            pairs = [
                part
                for i in (0, 2)
                for part in (
                    jnp.where(even, blocks[i], pltpu.roll(blocks[i + 1], KW, 1)),
                    jnp.where(even, pltpu.roll(blocks[i], LANES - KW, 1), blocks[i + 1]),
                )
            ]
            fields = [
                jnp.where(lower, pairs[0], pltpu.roll(pairs[2], LANES // 2, 1)),
                jnp.where(lower, pairs[1], pltpu.roll(pairs[3], LANES // 2, 1)),
                jnp.where(lower, pltpu.roll(pairs[0], LANES // 2, 1), pairs[2]),
                jnp.where(lower, pltpu.roll(pairs[1], LANES // 2, 1), pairs[3]),
            ]
            extra = jnp.zeros((rows - tail, LANES), jnp.float32)
            for i in range(2 * parts):
                k = i * quads + distance * members + half
                extra = jnp.where(row_id == capacity + i, labels[k : k + 1], extra)
            for f in range(F):
                message = jnp.concatenate([fields[f][:tail], fields[f][tail:] + extra], axis=0)
                if distance < NEAR:
                    near[distance][field ^ f, half] = message
                else:
                    by_field[distance - NEAR, half, f] = message
            if distance >= NEAR:
                for q in range(F):
                    far[q][distance - NEAR, half] = by_field[distance - NEAR, half, field ^ q]


def prepare_kernel(members, lon_cols, zonal, vert, zonal_high, zonal_low, vert_both, turned):
    position = lax.axis_index("lon")
    f, h = position // members, lax.rem(position, members)
    turned[...] = zonal[...].T
    for e in range(members):
        for q in range(F):
            block = (f ^ q) * members + lax.rem(h + e, members)
            part = turned[pl.ds(pl.multiple_of(block * lon_cols, lon_cols), lon_cols), :]
            at = slice((e * F + q) * lon_cols, (e * F + q + 1) * lon_cols)
            zonal_high[at], zonal_low[at] = split(part)
    high, low = split(vert[f])
    vert_both[:LEV, :LEV] = high
    vert_both[:LEV, LEV:] = low
    vert_both[LEV:, :LEV] = high
    vert_both[LEV:, LEV:] = jnp.zeros_like(low)


def scatter(pieces, half, capacity, columns):
    rows = pieces[0].shape[0]
    count = len(pieces)
    slots = -(-count * rows // LANES) * LANES
    parts, _ = message_rows(capacity)
    row_id, lane_id = iota((rows, LANES), 0), iota((rows, LANES), 1)
    piece_id = row_id >> (KW.bit_length() - 1)
    diagonal = ((lane_id & (KW - 1)) == (row_id & (KW - 1))) & (row_id < capacity)
    empty = jnp.where((row_id >= capacity) & ((lane_id & (KW - 1)) == 0), -1.0, 0.0)
    labels = []
    for piece in pieces:
        cell, offset = empty, jnp.zeros((rows, LANES), jnp.float32)
        for p in range(parts):
            mine = diagonal & (piece_id == p)
            at = capacity + 2 * p
            cell = jnp.where(mine, piece[at : at + 1], cell)
            offset = jnp.where(mine, piece[at + 1 : at + 2], offset)
        labels.append(jnp.concatenate([cell, offset], axis=1))
    spare = slots - count * rows
    if spare:
        pieces = pieces + [jnp.zeros((spare, LANES), jnp.float32)]
        labels.append(jnp.full((spare, 2 * LANES), -1.0, jnp.float32))
    picker = (
        iota((2 * GROUPS, 2 * LANES), 0) == iota((2 * GROUPS, 2 * LANES), 1) >> (KW.bit_length() - 1)
    ).astype(jnp.bfloat16)
    along = (((1,), (1,)), ((), ()))
    label_rows = lax.dot_general(
        picker,
        jnp.concatenate(labels, axis=0).astype(jnp.bfloat16),
        along,
        preferred_element_type=jnp.float32,
    ).astype(jnp.bfloat16)
    high, low = split(jnp.concatenate(pieces, axis=0).T)
    middle = iota((LEV, slots), 0).astype(jnp.bfloat16) - jnp.bfloat16((KW - 1) / 2)
    sums = []
    for g in range(GROUPS):
        at = slice(g * KW, (g + 1) * KW)
        inside = jnp.abs(middle - label_rows[GROUPS + g : GROUPS + g + 1]) < jnp.bfloat16(KW / 2)
        placed = jnp.concatenate(
            [
                jnp.where(inside, jnp.concatenate([piece[at]] * (LEV // KW), axis=0), jnp.bfloat16(0))
                for piece in (high, low)
            ],
            axis=0,
        )
        both = lax.dot_general(
            one_hot(label_rows[g : g + 1], columns),
            placed,
            along,
            preferred_element_type=jnp.float32,
        )
        sums.append(both[:, :LEV] + both[:, LEV:])
    return sums


def early_kernel(capacity, *refs):
    received, out = refs[:-1], refs[-1]
    halves, columns = received[0].shape[1], out.shape[1]
    for half in range(halves):
        pieces = [ref[k, half] for ref in received for k in range(ref.shape[0])]
        for g, total in enumerate(scatter(pieces, half, capacity, columns)):
            out[half * GROUPS + g] = total


def late_kernel(capacity, lon_cols, count, *refs):
    received = refs[:count]
    early, zonal_high, zonal_low, vert_both, high_out, low_out, *partials = refs[count:]
    halves, columns = received[0].shape[1], early.shape[1]
    for half in range(halves):
        pieces = [ref[k, half] for ref in received for k in range(ref.shape[0])]
        for g, total in enumerate(scatter(pieces, half, capacity, columns)):
            block = half * GROUPS + g
            adjoint_high, adjoint_low = split(early[block] + total)
            both = dot(jnp.concatenate([adjoint_high, adjoint_low], axis=1), vert_both[...])
            vertical = both[:, :LEV] + both[:, LEV:]
            high, low = split(vertical)
            for a in range(columns // lon_cols):
                at = slice(block * lon_cols, (block + 1) * lon_cols)
                rows = slice(a * lon_cols, (a + 1) * lon_cols)
                high_out[at, a * LEV : (a + 1) * LEV] = high[rows]
                low_out[at, a * LEV : (a + 1) * LEV] = low[rows]
    for e, partial in enumerate(partials, 1):
        partial[...] = zonal_product(e, zonal_high, zonal_low, high_out, low_out, partial.shape[0])


def zonal_product(e, zonal_high, zonal_low, high, low, size):
    at = slice(e * size, (e + 1) * size)
    first = dot(zonal_high[at], high[...]) + dot(zonal_low[at], high[...])
    return first + dot(zonal_high[at], low[...])


def own_kernel(zonal_high, zonal_low, high, low, out):
    out[...] = zonal_product(0, zonal_high, zonal_low, high, low, out.shape[0])


def sum_kernel(lon_cols, *refs):
    terms, outs = refs[:-F], refs[-F:]
    for q in range(F):
        at = slice(q * lon_cols, (q + 1) * lon_cols)
        total = terms[0][at]
        for term in terms[1:]:
            total = total + term[at]
        outs[q][...] = total


def finish_kernel(members, distances, *refs):
    count = len(distances)
    control, parts = refs[0], refs[1 : 1 + count]
    out, held, sent = refs[-3:]
    field = lax.axis_index("lon") // members
    copies = []
    for i, q in enumerate(distances):
        at = pl.ds(pl.multiple_of((field ^ q) * LEV, LEV), LEV)
        for a in range(control.shape[0]):
            held[i, a] = control[a, :, at] + parts[i][:, a * LEV : (a + 1) * LEV]
        copies.append(pltpu.make_async_copy(held.at[i], out.at[:, :, at], sent.at[i]))
        copies[-1].start()
    for copy in copies:
        copy.wait()


def call(kernel, out_shape, n_in, vmem=24, flops=0, nbytes=0, scratch=()):
    one = pl.BlockSpec(memory_space=pltpu.VMEM)
    return pl.pallas_call(
        kernel,
        out_shape=out_shape,
        in_specs=[one] * n_in,
        out_specs=[one] * len(out_shape) if isinstance(out_shape, (list, tuple)) else one,
        scratch_shapes=list(scratch),
        compiler_params=pltpu.CompilerParams(vmem_limit_bytes=vmem * MIB),
        cost_estimate=pl.CostEstimate(flops=flops, bytes_accessed=nbytes, transcendentals=0),
    )


def along_lat(x, d):
    lats = lax.axis_size("lat")
    return lax.ppermute(x, "lat", [(i, i ^ d ^ ((i & d & 2) >> 1)) for i in range(lats)])


def to_field(x, q, members):
    if q == 0:
        return x
    lons = lax.axis_size("lon")
    return lax.ppermute(
        x, "lon", [(i, (i // members ^ q) * members + i % members) for i in range(lons)]
    )


def to_member(x, e, members):
    lons = lax.axis_size("lon")
    return lax.ppermute(
        x, "lon", [(i, i // members * members + (i + e) % members) for i in range(lons)]
    )


def per_device(
    control,
    vert_factor,
    zonal_factor,
    obs_dest,
    obs_cell,
    obs_offset,
    obs_count,
    departure,
    obs_rinv,
    obs_weights,
):
    lats = lax.axis_size("lat")
    lons = lax.axis_size("lon")
    devices = lats * lons
    members = lons // F
    n_obs = obs_cell.shape[0]
    capacity = max(2, 3 * n_obs // (2 * devices))
    _, rows = message_rows(capacity)
    lat_rows, lon_cols, _ = control.shape
    columns = lat_rows * lon_cols
    blocks = lons
    all_lons = lons * lon_cols
    share = F * lon_cols
    wide = lat_rows * LEV
    f32, bf16 = jnp.float32, jnp.bfloat16
    far_messages = jax.ShapeDtypeStruct((lats - NEAR, members, rows, LANES), f32)
    near_messages = jax.ShapeDtypeStruct((F, members, rows, LANES), f32)
    messages = pl.pallas_call(
        functools.partial(pack_kernel, members, capacity, lats),
        out_shape=[far_messages] * F + [near_messages] * NEAR,
        in_specs=[pl.BlockSpec(memory_space=pltpu.HBM)] * 7,
        out_specs=[pl.BlockSpec(memory_space=pltpu.VMEM)] * (F + NEAR),
        scratch_shapes=[
            pltpu.SMEM((1, 1), jnp.int32),
            pltpu.VMEM((1, n_obs), jnp.int32),
            pltpu.VMEM((n_obs,), jnp.int32),
            pltpu.VMEM((n_obs,), jnp.int32),
            pltpu.VMEM((n_obs,), f32),
            pltpu.VMEM((n_obs,), f32),
            pltpu.VMEM((n_obs, LANES), f32),
            pltpu.VMEM((lats - NEAR, members, F, rows, LANES), f32),
            pltpu.SemaphoreType.DMA((7,)),
        ],
        compiler_params=pltpu.CompilerParams(vmem_limit_bytes=24 * MIB),
        cost_estimate=pl.CostEstimate(
            flops=4 * devices * rows * n_obs * LANES, bytes_accessed=1 << 20, transcendentals=0
        ),
    )(
        obs_count.reshape(1, 1),
        *(
            pltpu.with_memory_space_constraint(x, pltpu.HBM)
            for x in (
                obs_dest.reshape(1, n_obs),
                obs_cell,
                obs_offset,
                departure,
                obs_rinv,
                obs_weights,
            )
        )
    )
    far, near = list(messages[:F]), list(messages[F:])
    far = [to_field(far[q], q, members) for q in range(F)]
    late = [
        along_lat(jnp.stack([part[d - NEAR] for part in far]), d)
        for d in reversed(range(NEAR, lats))
    ]
    near = near[:1] + [along_lat(near[d], d) for d in range(1, NEAR)]
    near = [to_field(jnp.stack([part[q] for part in near]), q, members) for q in range(F)]
    zonal_high, zonal_low, vert_both = call(
        functools.partial(prepare_kernel, members, lon_cols),
        [
            jax.ShapeDtypeStruct((members * share, all_lons), bf16),
            jax.ShapeDtypeStruct((members * share, all_lons), bf16),
            jax.ShapeDtypeStruct((2 * LEV, 2 * LEV), bf16),
        ],
        2,
        scratch=[pltpu.VMEM(zonal_factor.shape, f32)],
        nbytes=2 << 20,
    )(zonal_factor, vert_factor)
    early = call(
        functools.partial(early_kernel, capacity),
        jax.ShapeDtypeStruct((blocks, columns, LEV), f32),
        F,
        vmem=24,
        flops=4 * blocks * columns * NEAR * F * rows * LEV,
        nbytes=2 << 20,
    )(*near)
    partial = jax.ShapeDtypeStruct((share, wide), f32)
    half_vertical = jax.ShapeDtypeStruct((all_lons, wide), bf16)
    high, low, *partials = call(
        functools.partial(late_kernel, capacity, lon_cols, len(late)),
        [half_vertical] * 2 + [partial] * (members - 1),
        4 + len(late),
        vmem=24,
        flops=6 * members * share * all_lons * wide,
        nbytes=2 << 20,
    )(*late, early, zonal_high, zonal_low, vert_both)
    others = [to_member(partials[e - 1], e, members) for e in range(1, members)]
    own = call(
        own_kernel, partial, 4, flops=6 * share * all_lons * wide, nbytes=1 << 20
    )(zonal_high, zonal_low, high, low)
    products = call(
        functools.partial(sum_kernel, lon_cols),
        [jax.ShapeDtypeStruct((lon_cols, wide), f32)] * F,
        members,
        nbytes=1 << 20,
    )(own, *others)
    parts = [to_field(products[q], q, members) for q in range(F)]
    out = ()
    for distances in ((0, 1), (2, 3)):
        count = len(distances)
        out = (
            pl.pallas_call(
                functools.partial(finish_kernel, members, distances),
                out_shape=jax.ShapeDtypeStruct(control.shape, f32),
                in_specs=[pl.BlockSpec(memory_space=pltpu.VMEM)] * (1 + count)
                + [pl.BlockSpec(memory_space=pltpu.HBM)] * len(out),
                out_specs=pl.BlockSpec(memory_space=pltpu.HBM),
                scratch_shapes=[
                    pltpu.VMEM((count, lat_rows, lon_cols, LEV), f32),
                    pltpu.SemaphoreType.DMA((count,)),
                ],
                input_output_aliases={1 + count: 0} if out else {},
                compiler_params=pltpu.CompilerParams(vmem_limit_bytes=24 * MIB),
                cost_estimate=pl.CostEstimate(
                    flops=0, bytes_accessed=count << 19, transcendentals=0
                ),
            )(control, *(parts[q] for q in distances), *out),
        )
    return out[0]


def solution(mesh):
    return jax.shard_map(
        per_device,
        mesh=mesh,
        in_specs=(
            P("lat", "lon", None),
            P(),
            P(),
            P(("lat", "lon"), None),
            P(("lat", "lon")),
            P(("lat", "lon")),
            P(("lat", "lon")),
            P(("lat", "lon")),
            P(("lat", "lon")),
            P(("lat", "lon"), None),
        ),
        out_specs=P("lat", "lon", None),
        check_vma=False,
    )
```

```python
import functools

import jax
import jax.numpy as jnp
from jax import lax
from jax.experimental import pallas as pl
from jax.experimental.pallas import tpu as pltpu
from jax.sharding import PartitionSpec as P

F = 4
LEV = 128
KW = 32
LANES = 128
SUBLANES = 8
GROUPS = LANES // KW
NEAR = 2
MIB = 1 << 20


def iota(shape, axis):
    return lax.broadcasted_iota(jnp.int32, shape, axis)


def split(x):
    high = x.astype(jnp.bfloat16)
    return high, (x - high.astype(jnp.float32)).astype(jnp.bfloat16)


def dot(a, b):
    return jnp.dot(a, b, preferred_element_type=jnp.float32)


def one_hot(labels, size):
    hit = iota((size, labels.shape[1]), 0).astype(jnp.bfloat16) == labels.astype(jnp.bfloat16)
    return jnp.where(hit, jnp.bfloat16(1), jnp.bfloat16(0))


def message_rows(capacity):
    parts = -(-capacity // KW)
    return parts, -(-(capacity + 2 * parts) // SUBLANES) * SUBLANES


def pack_kernel(members, capacity, lats, *refs):
    sources, far = refs[:7], refs[7 : 7 + F]
    quad_out, slot_out, pieces_out, labels_out = refs[7 + F : 11 + F]
    held, by_field, arrived = refs[11 + F : -2], refs[-2], refs[-1]
    far_bands = tuple(range(NEAR, lats))
    loads = [
        pltpu.make_async_copy(source, target, arrived.at[i])
        for i, (source, target) in enumerate(zip(sources, held))
    ]
    for i in (1, 6, 0, 2, 3, 4, 5):
        loads[i].start()
    count, dest, cell, offset, departure, rinv, weights = held
    n = weights.shape[0]
    rows = far[0].shape[2]
    lons = F * members
    devices = lats * lons
    field = lax.axis_index("lon") // members
    parts, _ = message_rows(capacity)
    quads = devices // GROUPS
    chunks = n // LANES
    loads[1].wait()
    lat = lax.axis_index("lat")
    band = dest[...] // lons ^ lat
    dest_row = (band ^ ((band & lat & 2) >> 1)) * lons + lax.rem(dest[...], lons)
    hits = [
        iota((devices, LANES), 0) == dest_row[:, c * LANES : (c + 1) * LANES] for c in range(chunks)
    ]
    stacked = jnp.concatenate([hit.astype(jnp.bfloat16) for hit in hits], axis=0)
    before = (iota((LANES, 2 * LANES), 0) < iota((LANES, 2 * LANES), 1)).astype(jnp.bfloat16)
    counts = dot(stacked, before)
    carry = jnp.zeros((devices, LANES), jnp.float32)
    ranks = []
    for c in range(chunks):
        part = counts[c * devices : (c + 1) * devices]
        ranks.append(
            jnp.sum(jnp.where(hits[c], part[:, :LANES] + carry, 0.0), axis=0, keepdims=True)
        )
        carry = carry + part[:, LANES:]
    rank = jnp.concatenate(ranks, axis=1).astype(jnp.int32)
    group = dest_row & (GROUPS - 1)
    quad = dest_row >> (GROUPS.bit_length() - 1)
    slot = group * rows + rank
    lane = group * KW + (rank & (KW - 1))
    piece = rank >> (KW.bit_length() - 1)
    for i in (0, 2, 3, 4, 5):
        loads[i].wait()
    cell_row, offset_row = cell[...].reshape(1, n), offset[...].reshape(1, n)
    live = iota((1, n), 1) < count[0, 0]
    scaled = jnp.where(
        live, rinv[...].reshape(1, n) * departure[...].reshape(1, n), jnp.float32(0.0)
    )
    columns = jnp.concatenate(
        [scaled, offset_row.astype(jnp.float32), jnp.zeros((SUBLANES - 2, n), jnp.float32)], axis=0
    ).T
    lane_id = iota((n, LANES), 1)
    label_rows = []
    for p in range(parts):
        for label in (cell_row, offset_row):
            mine = (iota((quads, n), 0) == quad) & (piece == p)
            label_rows.append(jnp.where(mine, label.astype(jnp.float32), 0.0))
    labels = lax.dot_general(
        jnp.concatenate(label_rows, axis=0).astype(jnp.bfloat16),
        one_hot(lane, LANES),
        (((1,), (1,)), ((), ())),
        preferred_element_type=jnp.float32,
    )
    source = (lane_id & -KW) | ((lane_id - columns[:, 1:2].astype(jnp.int32)) & (KW - 1))
    loads[6].wait()
    turned = jnp.take_along_axis(weights[...], source, axis=1, mode="promise_in_bounds")
    high, low = split(turned * columns[:, 0:1])
    pieces = jnp.concatenate([high, low], axis=1)
    form_messages(
        far_bands, capacity, members, quads, rows, quad, slot, pieces, labels, by_field
    )
    for k in range(len(far_bands)):
        for half in range(members):
            for q in range(F):
                far[q][k, half] = by_field[field ^ q, k, half]
    quad_out[...], slot_out[...] = quad, slot
    pieces_out[...], labels_out[...] = pieces, labels


def near_kernel(capacity, members, quad, slot, pieces, labels, *outs):
    rows = outs[0].shape[2]
    by_field = outs[-1]
    outs = outs[:-1]
    quads = labels.shape[0] // (2 * message_rows(capacity)[0])
    field = lax.axis_index("lon") // members
    bands = tuple(reversed(range(NEAR)))
    form_messages(
        bands, capacity, members, quads, rows, quad[...], slot[...], pieces[...], labels[...], by_field
    )
    for k, distance in enumerate(bands):
        for half in range(members):
            for q in range(F):
                outs[distance][q, half] = by_field[field ^ q, k, half]


def form_messages(
    bands, capacity, members, quads, rows, quad, slot, pieces, labels, by_field
):
    parts, _ = message_rows(capacity)
    even = iota((rows, LANES), 1) & KW == 0
    lower = iota((rows, LANES), 1) < LANES // 2
    size = GROUPS * rows
    tail = capacity // SUBLANES * SUBLANES
    row_id = iota((rows - tail, LANES), 0) + tail
    hits = jnp.concatenate(
        [
            one_hot(jnp.where(quad == distance * members + half, slot, -1), size)
            for distance in bands
            for half in range(members)
        ],
        axis=0,
    )
    both = dot(hits, pieces)
    for step, distance in enumerate(bands):
        for half in range(members):
            at = (step * members + half) * size
            picked = both[at : at + size, :LANES] + both[at : at + size, LANES:]
            blocks = [picked[g * rows : (g + 1) * rows] for g in range(GROUPS)]
            pairs = [
                part
                for i in (0, 2)
                for part in (
                    jnp.where(even, blocks[i], pltpu.roll(blocks[i + 1], KW, 1)),
                    jnp.where(even, pltpu.roll(blocks[i], LANES - KW, 1), blocks[i + 1]),
                )
            ]
            fields = [
                jnp.where(lower, pairs[0], pltpu.roll(pairs[2], LANES // 2, 1)),
                jnp.where(lower, pairs[1], pltpu.roll(pairs[3], LANES // 2, 1)),
                jnp.where(lower, pltpu.roll(pairs[0], LANES // 2, 1), pairs[2]),
                jnp.where(lower, pltpu.roll(pairs[1], LANES // 2, 1), pairs[3]),
            ]
            extra = jnp.zeros((rows - tail, LANES), jnp.float32)
            for i in range(2 * parts):
                k = i * quads + distance * members + half
                extra = jnp.where(row_id == capacity + i, labels[k : k + 1], extra)
            for f in range(F):
                by_field[f, step, half] = jnp.concatenate(
                    [fields[f][:tail], fields[f][tail:] + extra], axis=0
                )


def prepare_kernel(members, lon_cols, zonal, vert, zonal_high, zonal_low, vert_both, turned):
    position = lax.axis_index("lon")
    f, h = position // members, lax.rem(position, members)
    turned[...] = zonal[...].T
    for e in range(members):
        for q in range(F):
            block = (f ^ q) * members + lax.rem(h + e, members)
            part = turned[pl.ds(pl.multiple_of(block * lon_cols, lon_cols), lon_cols), :]
            at = slice((e * F + q) * lon_cols, (e * F + q + 1) * lon_cols)
            zonal_high[at], zonal_low[at] = split(part)
    high, low = split(vert[f])
    vert_both[:LEV, :LEV] = high
    vert_both[:LEV, LEV:] = low
    vert_both[LEV:, :LEV] = high
    vert_both[LEV:, LEV:] = jnp.zeros_like(low)


def scatter(pieces, half, capacity, columns):
    rows = pieces[0].shape[0]
    count = len(pieces)
    slots = -(-count * rows // LANES) * LANES
    parts, _ = message_rows(capacity)
    row_id, lane_id = iota((rows, LANES), 0), iota((rows, LANES), 1)
    piece_id = row_id >> (KW.bit_length() - 1)
    diagonal = ((lane_id & (KW - 1)) == (row_id & (KW - 1))) & (row_id < capacity)
    empty = jnp.where((row_id >= capacity) & ((lane_id & (KW - 1)) == 0), -1.0, 0.0)
    labels = []
    for piece in pieces:
        cell, offset = empty, jnp.zeros((rows, LANES), jnp.float32)
        for p in range(parts):
            mine = diagonal & (piece_id == p)
            at = capacity + 2 * p
            cell = jnp.where(mine, piece[at : at + 1], cell)
            offset = jnp.where(mine, piece[at + 1 : at + 2], offset)
        labels.append(jnp.concatenate([cell, offset], axis=1))
    spare = slots - count * rows
    if spare:
        pieces = pieces + [jnp.zeros((spare, LANES), jnp.float32)]
        labels.append(jnp.full((spare, 2 * LANES), -1.0, jnp.float32))
    picker = (
        iota((2 * GROUPS, 2 * LANES), 0) == iota((2 * GROUPS, 2 * LANES), 1) >> (KW.bit_length() - 1)
    ).astype(jnp.bfloat16)
    along = (((1,), (1,)), ((), ()))
    label_rows = lax.dot_general(
        picker,
        jnp.concatenate(labels, axis=0).astype(jnp.bfloat16),
        along,
        preferred_element_type=jnp.float32,
    ).astype(jnp.bfloat16)
    high, low = split(jnp.concatenate(pieces, axis=0).T)
    middle = iota((LEV, slots), 0).astype(jnp.bfloat16) - jnp.bfloat16((KW - 1) / 2)
    sums = []
    for g in range(GROUPS):
        at = slice(g * KW, (g + 1) * KW)
        inside = jnp.abs(middle - label_rows[GROUPS + g : GROUPS + g + 1]) < jnp.bfloat16(KW / 2)
        placed = jnp.concatenate(
            [
                jnp.where(inside, jnp.concatenate([piece[at]] * (LEV // KW), axis=0), jnp.bfloat16(0))
                for piece in (high, low)
            ],
            axis=0,
        )
        both = lax.dot_general(
            one_hot(label_rows[g : g + 1], columns),
            placed,
            along,
            preferred_element_type=jnp.float32,
        )
        sums.append(both[:, :LEV] + both[:, LEV:])
    return sums


def early_kernel(capacity, *refs):
    received, out = refs[:-1], refs[-1]
    halves, columns = received[0].shape[1], out.shape[1]
    for half in range(halves):
        pieces = [ref[k, half] for ref in received for k in range(ref.shape[0])]
        for g, total in enumerate(scatter(pieces, half, capacity, columns)):
            out[half * GROUPS + g] = total


def late_kernel(capacity, lon_cols, count, *refs):
    received = refs[:count]
    early, zonal_high, zonal_low, vert_both, high_out, low_out, *partials = refs[count:]
    halves, columns = received[0].shape[1], early.shape[1]
    for half in range(halves):
        pieces = [ref[k, half] for ref in received for k in range(ref.shape[0])]
        for g, total in enumerate(scatter(pieces, half, capacity, columns)):
            block = half * GROUPS + g
            adjoint_high, adjoint_low = split(early[block] + total)
            both = dot(jnp.concatenate([adjoint_high, adjoint_low], axis=1), vert_both[...])
            vertical = both[:, :LEV] + both[:, LEV:]
            high, low = split(vertical)
            for a in range(columns // lon_cols):
                at = slice(block * lon_cols, (block + 1) * lon_cols)
                rows = slice(a * lon_cols, (a + 1) * lon_cols)
                high_out[at, a * LEV : (a + 1) * LEV] = high[rows]
                low_out[at, a * LEV : (a + 1) * LEV] = low[rows]
    for e, partial in enumerate(partials, 1):
        partial[...] = zonal_product(e, zonal_high, zonal_low, high_out, low_out, partial.shape[0])


def zonal_product(e, zonal_high, zonal_low, high, low, size):
    at = slice(e * size, (e + 1) * size)
    first = dot(zonal_high[at], high[...]) + dot(zonal_low[at], high[...])
    return first + dot(zonal_high[at], low[...])


def own_kernel(zonal_high, zonal_low, high, low, out):
    out[...] = zonal_product(0, zonal_high, zonal_low, high, low, out.shape[0])


def sum_kernel(lon_cols, *refs):
    terms, outs = refs[:-F], refs[-F:]
    for q in range(F):
        at = slice(q * lon_cols, (q + 1) * lon_cols)
        total = terms[0][at]
        for term in terms[1:]:
            total = total + term[at]
        outs[q][...] = total


def finish_kernel(members, distances, *refs):
    count = len(distances)
    control, parts = refs[0], refs[1 : 1 + count]
    out, held, sent = refs[-3:]
    field = lax.axis_index("lon") // members
    copies = []
    for i, q in enumerate(distances):
        at = pl.ds(pl.multiple_of((field ^ q) * LEV, LEV), LEV)
        for a in range(control.shape[0]):
            held[i, a] = control[a, :, at] + parts[i][:, a * LEV : (a + 1) * LEV]
        copies.append(pltpu.make_async_copy(held.at[i], out.at[:, :, at], sent.at[i]))
        copies[-1].start()
    for copy in copies:
        copy.wait()


def call(kernel, out_shape, n_in, vmem=24, flops=0, nbytes=0, scratch=()):
    one = pl.BlockSpec(memory_space=pltpu.VMEM)
    return pl.pallas_call(
        kernel,
        out_shape=out_shape,
        in_specs=[one] * n_in,
        out_specs=[one] * len(out_shape) if isinstance(out_shape, (list, tuple)) else one,
        scratch_shapes=list(scratch),
        compiler_params=pltpu.CompilerParams(vmem_limit_bytes=vmem * MIB),
        cost_estimate=pl.CostEstimate(flops=flops, bytes_accessed=nbytes, transcendentals=0),
    )


def along_lat(x, d):
    lats = lax.axis_size("lat")
    return lax.ppermute(x, "lat", [(i, i ^ d ^ ((i & d & 2) >> 1)) for i in range(lats)])


def to_field(x, q, members):
    if q == 0:
        return x
    lons = lax.axis_size("lon")
    return lax.ppermute(
        x, "lon", [(i, (i // members ^ q) * members + i % members) for i in range(lons)]
    )


def to_member(x, e, members):
    lons = lax.axis_size("lon")
    return lax.ppermute(
        x, "lon", [(i, i // members * members + (i + e) % members) for i in range(lons)]
    )


def per_device(
    control,
    vert_factor,
    zonal_factor,
    obs_dest,
    obs_cell,
    obs_offset,
    obs_count,
    departure,
    obs_rinv,
    obs_weights,
):
    lats = lax.axis_size("lat")
    lons = lax.axis_size("lon")
    devices = lats * lons
    members = lons // F
    n_obs = obs_cell.shape[0]
    capacity = max(2, 3 * n_obs // (2 * devices))
    parts, rows = message_rows(capacity)
    lat_rows, lon_cols, _ = control.shape
    columns = lat_rows * lon_cols
    blocks = lons
    all_lons = lons * lon_cols
    share = F * lon_cols
    wide = lat_rows * LEV
    f32, bf16 = jnp.float32, jnp.bfloat16
    far_messages = jax.ShapeDtypeStruct((lats - NEAR, members, rows, LANES), f32)
    near_messages = jax.ShapeDtypeStruct((F, members, rows, LANES), f32)
    messages = pl.pallas_call(
        functools.partial(pack_kernel, members, capacity, lats),
        out_shape=[far_messages] * F
        + [
            jax.ShapeDtypeStruct((1, n_obs), jnp.int32),
            jax.ShapeDtypeStruct((1, n_obs), jnp.int32),
            jax.ShapeDtypeStruct((n_obs, 2 * LANES), bf16),
            jax.ShapeDtypeStruct((2 * parts * devices // GROUPS, LANES), f32),
        ],
        in_specs=[pl.BlockSpec(memory_space=pltpu.HBM)] * 7,
        out_specs=[pl.BlockSpec(memory_space=pltpu.VMEM)] * (F + 4),
        scratch_shapes=[
            pltpu.SMEM((1, 1), jnp.int32),
            pltpu.VMEM((1, n_obs), jnp.int32),
            pltpu.VMEM((n_obs,), jnp.int32),
            pltpu.VMEM((n_obs,), jnp.int32),
            pltpu.VMEM((n_obs,), f32),
            pltpu.VMEM((n_obs,), f32),
            pltpu.VMEM((n_obs, LANES), f32),
            pltpu.VMEM((F, lats - NEAR, members, rows, LANES), f32),
            pltpu.SemaphoreType.DMA((7,)),
        ],
        compiler_params=pltpu.CompilerParams(vmem_limit_bytes=24 * MIB),
        cost_estimate=pl.CostEstimate(
            flops=4 * devices * rows * n_obs * LANES, bytes_accessed=1 << 20, transcendentals=0
        ),
    )(
        obs_count.reshape(1, 1),
        *(
            pltpu.with_memory_space_constraint(x, pltpu.HBM)
            for x in (
                obs_dest.reshape(1, n_obs),
                obs_cell,
                obs_offset,
                departure,
                obs_rinv,
                obs_weights,
            )
        )
    )
    far = [to_field(messages[q], q, members) for q in range(F)]
    near = list(
        call(
            functools.partial(near_kernel, capacity, members),
            [near_messages] * NEAR,
            4,
            scratch=[pltpu.VMEM((F, NEAR, members, rows, LANES), f32)],
            flops=4 * NEAR * members * GROUPS * rows * n_obs * LANES,
            nbytes=1 << 20,
        )(*messages[F:])
    )
    late = [
        along_lat(jnp.stack([part[d - NEAR] for part in far]), d)
        for d in reversed(range(NEAR, lats))
    ]
    near = near[:1] + [along_lat(near[d], d) for d in range(1, NEAR)]
    near = [to_field(jnp.stack([part[q] for part in near]), q, members) for q in range(F)]
    zonal_high, zonal_low, vert_both = call(
        functools.partial(prepare_kernel, members, lon_cols),
        [
            jax.ShapeDtypeStruct((members * share, all_lons), bf16),
            jax.ShapeDtypeStruct((members * share, all_lons), bf16),
            jax.ShapeDtypeStruct((2 * LEV, 2 * LEV), bf16),
        ],
        2,
        scratch=[pltpu.VMEM(zonal_factor.shape, f32)],
        nbytes=2 << 20,
    )(zonal_factor, vert_factor)
    early = call(
        functools.partial(early_kernel, capacity),
        jax.ShapeDtypeStruct((blocks, columns, LEV), f32),
        F,
        vmem=24,
        flops=4 * blocks * columns * NEAR * F * rows * LEV,
        nbytes=2 << 20,
    )(*near)
    partial = jax.ShapeDtypeStruct((share, wide), f32)
    half_vertical = jax.ShapeDtypeStruct((all_lons, wide), bf16)
    high, low, *partials = call(
        functools.partial(late_kernel, capacity, lon_cols, len(late)),
        [half_vertical] * 2 + [partial] * (members - 1),
        4 + len(late),
        vmem=24,
        flops=6 * members * share * all_lons * wide,
        nbytes=2 << 20,
    )(*late, early, zonal_high, zonal_low, vert_both)
    others = [to_member(partials[e - 1], e, members) for e in range(1, members)]
    own = call(
        own_kernel, partial, 4, flops=6 * share * all_lons * wide, nbytes=1 << 20
    )(zonal_high, zonal_low, high, low)
    products = call(
        functools.partial(sum_kernel, lon_cols),
        [jax.ShapeDtypeStruct((lon_cols, wide), f32)] * F,
        members,
        nbytes=1 << 20,
    )(own, *others)
    parts = [to_field(products[q], q, members) for q in range(F)]
    out = ()
    for distances in ((0, 1), (2, 3)):
        count = len(distances)
        out = (
            pl.pallas_call(
                functools.partial(finish_kernel, members, distances),
                out_shape=jax.ShapeDtypeStruct(control.shape, f32),
                in_specs=[pl.BlockSpec(memory_space=pltpu.VMEM)] * (1 + count)
                + [pl.BlockSpec(memory_space=pltpu.HBM)] * len(out),
                out_specs=pl.BlockSpec(memory_space=pltpu.HBM),
                scratch_shapes=[
                    pltpu.VMEM((count, lat_rows, lon_cols, LEV), f32),
                    pltpu.SemaphoreType.DMA((count,)),
                ],
                input_output_aliases={1 + count: 0} if out else {},
                compiler_params=pltpu.CompilerParams(vmem_limit_bytes=24 * MIB),
                cost_estimate=pl.CostEstimate(
                    flops=0, bytes_accessed=count << 19, transcendentals=0
                ),
            )(control, *(parts[q] for q in distances), *out),
        )
    return out[0]


def solution(mesh):
    return jax.shard_map(
        per_device,
        mesh=mesh,
        in_specs=(
            P("lat", "lon", None),
            P(),
            P(),
            P(("lat", "lon"), None),
            P(("lat", "lon")),
            P(("lat", "lon")),
            P(("lat", "lon")),
            P(("lat", "lon")),
            P(("lat", "lon")),
            P(("lat", "lon"), None),
        ),
        out_specs=P("lat", "lon", None),
        check_vma=False,
    )
```

```python
import functools

import jax
import jax.numpy as jnp
from jax import lax
from jax.experimental import pallas as pl
from jax.experimental.pallas import tpu as pltpu
from jax.sharding import PartitionSpec as P

F = 4
LEV = 128
KW = 32
LANES = 128
SUBLANES = 8
GROUPS = LANES // KW
NEAR = 2
MIB = 1 << 20


def iota(shape, axis):
    return lax.broadcasted_iota(jnp.int32, shape, axis)


def split(x):
    high = x.astype(jnp.bfloat16)
    return high, (x - high.astype(jnp.float32)).astype(jnp.bfloat16)


def dot(a, b):
    return jnp.dot(a, b, preferred_element_type=jnp.float32)


def one_hot(labels, size):
    hit = iota((size, labels.shape[1]), 0).astype(jnp.bfloat16) == labels.astype(jnp.bfloat16)
    return jnp.where(hit, jnp.bfloat16(1), jnp.bfloat16(0))


def message_rows(capacity):
    parts = -(-capacity // KW)
    return parts, -(-(capacity + 2 * parts) // SUBLANES) * SUBLANES


def pack_kernel(members, capacity, lats, *refs):
    sources, far, near = refs[:7], refs[7 : 7 + F], refs[7 + F : 7 + F + NEAR]
    held, by_field, arrived = refs[7 + F + NEAR : -2], refs[-2], refs[-1]
    loads = [
        pltpu.make_async_copy(source, target, arrived.at[i])
        for i, (source, target) in enumerate(zip(sources, held))
    ]
    for i in (1, 6, 0, 2, 3, 4, 5):
        loads[i].start()
    count, dest, cell, offset, departure, rinv, weights = held
    n = weights.shape[0]
    rows = far[0].shape[2]
    lons = F * members
    devices = lats * lons
    field = lax.axis_index("lon") // members
    parts, _ = message_rows(capacity)
    quads = devices // GROUPS
    chunks = n // LANES
    loads[1].wait()
    lat = lax.axis_index("lat")
    band = dest[...] // lons ^ lat
    dest_row = (band ^ ((band & lat & 2) >> 1)) * lons + lax.rem(dest[...], lons)
    hits = [
        iota((devices, LANES), 0) == dest_row[:, c * LANES : (c + 1) * LANES] for c in range(chunks)
    ]
    stacked = jnp.concatenate([hit.astype(jnp.bfloat16) for hit in hits], axis=0)
    before = (iota((LANES, 2 * LANES), 0) < iota((LANES, 2 * LANES), 1)).astype(jnp.bfloat16)
    counts = dot(stacked, before)
    carry = jnp.zeros((devices, LANES), jnp.float32)
    ranks = []
    for c in range(chunks):
        part = counts[c * devices : (c + 1) * devices]
        ranks.append(
            jnp.sum(jnp.where(hits[c], part[:, :LANES] + carry, 0.0), axis=0, keepdims=True)
        )
        carry = carry + part[:, LANES:]
    rank = jnp.concatenate(ranks, axis=1).astype(jnp.int32)
    group = dest_row & (GROUPS - 1)
    quad = dest_row >> (GROUPS.bit_length() - 1)
    slot = group * rows + rank
    lane = group * KW + (rank & (KW - 1))
    piece = rank >> (KW.bit_length() - 1)
    for i in (0, 2, 3, 4, 5):
        loads[i].wait()
    cell_row, offset_row = cell[...].reshape(1, n), offset[...].reshape(1, n)
    live = iota((1, n), 1) < count[0, 0]
    scaled = jnp.where(
        live, rinv[...].reshape(1, n) * departure[...].reshape(1, n), jnp.float32(0.0)
    )
    columns = jnp.concatenate(
        [scaled, offset_row.astype(jnp.float32), jnp.zeros((SUBLANES - 2, n), jnp.float32)], axis=0
    ).T
    lane_id = iota((n, LANES), 1)
    label_rows = []
    for p in range(parts):
        for label in (cell_row, offset_row):
            mine = (iota((quads, n), 0) == quad) & (piece == p)
            label_rows.append(jnp.where(mine, label.astype(jnp.float32), 0.0))
    labels = lax.dot_general(
        jnp.concatenate(label_rows, axis=0).astype(jnp.bfloat16),
        one_hot(lane, LANES),
        (((1,), (1,)), ((), ())),
        preferred_element_type=jnp.float32,
    )
    source = (lane_id & -KW) | ((lane_id - columns[:, 1:2].astype(jnp.int32)) & (KW - 1))
    loads[6].wait()
    turned = jnp.take_along_axis(weights[...], source, axis=1, mode="promise_in_bounds")
    high, low = split(turned * columns[:, 0:1])
    pieces = jnp.concatenate([high, low], axis=1)
    even = iota((rows, LANES), 1) & KW == 0
    lower = iota((rows, LANES), 1) < LANES // 2
    size = GROUPS * rows
    tail = capacity // SUBLANES * SUBLANES
    row_id = iota((rows - tail, LANES), 0) + tail
    order = (*range(NEAR, lats), *reversed(range(NEAR)))
    products = [
        dot(
            jnp.concatenate(
                [
                    one_hot(jnp.where(quad == distance * members + half, slot, -1), size)
                    for distance in bands
                    for half in range(members)
                ],
                axis=0,
            ),
            pieces,
        )
        for bands in (order[: lats - NEAR], order[lats - NEAR :])
    ]
    both = jnp.concatenate(products, axis=0)
    for step, distance in enumerate(order):
        for half in range(members):
            at = (step * members + half) * size
            picked = both[at : at + size, :LANES] + both[at : at + size, LANES:]
            blocks = [picked[g * rows : (g + 1) * rows] for g in range(GROUPS)]
            pairs = [
                part
                for i in (0, 2)
                for part in (
                    jnp.where(even, blocks[i], pltpu.roll(blocks[i + 1], KW, 1)),
                    jnp.where(even, pltpu.roll(blocks[i], LANES - KW, 1), blocks[i + 1]),
                )
            ]
            fields = [
                jnp.where(lower, pairs[0], pltpu.roll(pairs[2], LANES // 2, 1)),
                jnp.where(lower, pairs[1], pltpu.roll(pairs[3], LANES // 2, 1)),
                jnp.where(lower, pltpu.roll(pairs[0], LANES // 2, 1), pairs[2]),
                jnp.where(lower, pltpu.roll(pairs[1], LANES // 2, 1), pairs[3]),
            ]
            extra = jnp.zeros((rows - tail, LANES), jnp.float32)
            for i in range(2 * parts):
                k = i * quads + distance * members + half
                extra = jnp.where(row_id == capacity + i, labels[k : k + 1], extra)
            for f in range(F):
                message = jnp.concatenate([fields[f][:tail], fields[f][tail:] + extra], axis=0)
                if distance < NEAR:
                    near[distance][field ^ f, half] = message
                else:
                    by_field[distance - NEAR, half, f] = message
            if distance >= NEAR:
                for q in range(F):
                    far[q][distance - NEAR, half] = by_field[distance - NEAR, half, field ^ q]


def prepare_kernel(members, lon_cols, zonal, vert, zonal_high, zonal_low, vert_both, turned):
    position = lax.axis_index("lon")
    f, h = position // members, lax.rem(position, members)
    turned[...] = zonal[...].T
    for e in range(members):
        for q in range(F):
            block = (f ^ q) * members + lax.rem(h + e, members)
            part = turned[pl.ds(pl.multiple_of(block * lon_cols, lon_cols), lon_cols), :]
            at = slice((e * F + q) * lon_cols, (e * F + q + 1) * lon_cols)
            zonal_high[at], zonal_low[at] = split(part)
    high, low = split(vert[f])
    vert_both[:LEV, :LEV] = high
    vert_both[:LEV, LEV:] = low
    vert_both[LEV:, :LEV] = high
    vert_both[LEV:, LEV:] = jnp.zeros_like(low)


def scatter(pieces, half, capacity, columns):
    rows = pieces[0].shape[0]
    count = len(pieces)
    slots = -(-count * rows // LANES) * LANES
    parts, _ = message_rows(capacity)
    row_id, lane_id = iota((rows, LANES), 0), iota((rows, LANES), 1)
    piece_id = row_id >> (KW.bit_length() - 1)
    diagonal = ((lane_id & (KW - 1)) == (row_id & (KW - 1))) & (row_id < capacity)
    empty = jnp.where((row_id >= capacity) & ((lane_id & (KW - 1)) == 0), -1.0, 0.0)
    labels = []
    for piece in pieces:
        cell, offset = empty, jnp.zeros((rows, LANES), jnp.float32)
        for p in range(parts):
            mine = diagonal & (piece_id == p)
            at = capacity + 2 * p
            cell = jnp.where(mine, piece[at : at + 1], cell)
            offset = jnp.where(mine, piece[at + 1 : at + 2], offset)
        labels.append(jnp.concatenate([cell, offset], axis=1))
    spare = slots - count * rows
    if spare:
        pieces = pieces + [jnp.zeros((spare, LANES), jnp.float32)]
        labels.append(jnp.full((spare, 2 * LANES), -1.0, jnp.float32))
    picker = (
        iota((2 * GROUPS, 2 * LANES), 0) == iota((2 * GROUPS, 2 * LANES), 1) >> (KW.bit_length() - 1)
    ).astype(jnp.bfloat16)
    along = (((1,), (1,)), ((), ()))
    label_rows = lax.dot_general(
        picker,
        jnp.concatenate(labels, axis=0).astype(jnp.bfloat16),
        along,
        preferred_element_type=jnp.float32,
    ).astype(jnp.bfloat16)
    high, low = split(jnp.concatenate(pieces, axis=0).T)
    middle = iota((LEV, slots), 0).astype(jnp.bfloat16) - jnp.bfloat16((KW - 1) / 2)
    sums = []
    for g in range(GROUPS):
        at = slice(g * KW, (g + 1) * KW)
        inside = jnp.abs(middle - label_rows[GROUPS + g : GROUPS + g + 1]) < jnp.bfloat16(KW / 2)
        placed = jnp.concatenate(
            [
                jnp.where(inside, jnp.concatenate([piece[at]] * (LEV // KW), axis=0), jnp.bfloat16(0))
                for piece in (high, low)
            ],
            axis=0,
        )
        both = lax.dot_general(
            one_hot(label_rows[g : g + 1], columns),
            placed,
            along,
            preferred_element_type=jnp.float32,
        )
        sums.append(both[:, :LEV] + both[:, LEV:])
    return sums


def early_kernel(capacity, *refs):
    received, out = refs[:-1], refs[-1]
    halves, columns = received[0].shape[1], out.shape[1]
    for half in range(halves):
        pieces = [ref[k, half] for ref in received for k in range(ref.shape[0])]
        for g, total in enumerate(scatter(pieces, half, capacity, columns)):
            out[half * GROUPS + g] = total


def late_kernel(capacity, lon_cols, count, *refs):
    received = refs[:count]
    early, zonal_high, zonal_low, vert_both, high_out, low_out, *partials = refs[count:]
    halves, columns = received[0].shape[1], early.shape[1]
    for half in range(halves):
        pieces = [ref[k, half] for ref in received for k in range(ref.shape[0])]
        for g, total in enumerate(scatter(pieces, half, capacity, columns)):
            block = half * GROUPS + g
            adjoint_high, adjoint_low = split(early[block] + total)
            both = dot(jnp.concatenate([adjoint_high, adjoint_low], axis=1), vert_both[...])
            vertical = both[:, :LEV] + both[:, LEV:]
            high, low = split(vertical)
            for a in range(columns // lon_cols):
                at = slice(block * lon_cols, (block + 1) * lon_cols)
                rows = slice(a * lon_cols, (a + 1) * lon_cols)
                high_out[at, a * LEV : (a + 1) * LEV] = high[rows]
                low_out[at, a * LEV : (a + 1) * LEV] = low[rows]
    for e, partial in enumerate(partials, 1):
        partial[...] = zonal_product(e, zonal_high, zonal_low, high_out, low_out, partial.shape[0])


def zonal_product(e, zonal_high, zonal_low, high, low, size):
    at = slice(e * size, (e + 1) * size)
    first = dot(zonal_high[at], high[...]) + dot(zonal_low[at], high[...])
    return first + dot(zonal_high[at], low[...])


def own_kernel(zonal_high, zonal_low, high, low, out):
    out[...] = zonal_product(0, zonal_high, zonal_low, high, low, out.shape[0])


def sum_kernel(lon_cols, *refs):
    terms, outs = refs[:-F], refs[-F:]
    for q in range(F):
        at = slice(q * lon_cols, (q + 1) * lon_cols)
        total = terms[0][at]
        for term in terms[1:]:
            total = total + term[at]
        outs[q][...] = total


def finish_kernel(members, distances, *refs):
    count = len(distances)
    control, parts = refs[0], refs[1 : 1 + count]
    out, held, sent = refs[-3:]
    field = lax.axis_index("lon") // members
    copies = []
    for i, q in enumerate(distances):
        at = pl.ds(pl.multiple_of((field ^ q) * LEV, LEV), LEV)
        for a in range(control.shape[0]):
            held[i, a] = control[a, :, at] + parts[i][:, a * LEV : (a + 1) * LEV]
        copies.append(pltpu.make_async_copy(held.at[i], out.at[:, :, at], sent.at[i]))
        copies[-1].start()
    for copy in copies:
        copy.wait()


def call(kernel, out_shape, n_in, vmem=24, flops=0, nbytes=0, scratch=()):
    one = pl.BlockSpec(memory_space=pltpu.VMEM)
    return pl.pallas_call(
        kernel,
        out_shape=out_shape,
        in_specs=[one] * n_in,
        out_specs=[one] * len(out_shape) if isinstance(out_shape, (list, tuple)) else one,
        scratch_shapes=list(scratch),
        compiler_params=pltpu.CompilerParams(vmem_limit_bytes=vmem * MIB),
        cost_estimate=pl.CostEstimate(flops=flops, bytes_accessed=nbytes, transcendentals=0),
    )


def along_lat(x, d):
    lats = lax.axis_size("lat")
    return lax.ppermute(x, "lat", [(i, i ^ d ^ ((i & d & 2) >> 1)) for i in range(lats)])


def to_field(x, q, members):
    if q == 0:
        return x
    lons = lax.axis_size("lon")
    return lax.ppermute(
        x, "lon", [(i, (i // members ^ q) * members + i % members) for i in range(lons)]
    )


def to_member(x, e, members):
    lons = lax.axis_size("lon")
    return lax.ppermute(
        x, "lon", [(i, i // members * members + (i + e) % members) for i in range(lons)]
    )


def per_device(
    control,
    vert_factor,
    zonal_factor,
    obs_dest,
    obs_cell,
    obs_offset,
    obs_count,
    departure,
    obs_rinv,
    obs_weights,
):
    lats = lax.axis_size("lat")
    lons = lax.axis_size("lon")
    devices = lats * lons
    members = lons // F
    n_obs = obs_cell.shape[0]
    capacity = max(2, 3 * n_obs // (2 * devices))
    _, rows = message_rows(capacity)
    lat_rows, lon_cols, _ = control.shape
    columns = lat_rows * lon_cols
    blocks = lons
    all_lons = lons * lon_cols
    share = F * lon_cols
    wide = lat_rows * LEV
    f32, bf16 = jnp.float32, jnp.bfloat16
    far_messages = jax.ShapeDtypeStruct((lats - NEAR, members, rows, LANES), f32)
    near_messages = jax.ShapeDtypeStruct((F, members, rows, LANES), f32)
    messages = pl.pallas_call(
        functools.partial(pack_kernel, members, capacity, lats),
        out_shape=[far_messages] * F + [near_messages] * NEAR,
        in_specs=[pl.BlockSpec(memory_space=pltpu.HBM)] * 7,
        out_specs=[pl.BlockSpec(memory_space=pltpu.VMEM)] * (F + NEAR),
        scratch_shapes=[
            pltpu.SMEM((1, 1), jnp.int32),
            pltpu.VMEM((1, n_obs), jnp.int32),
            pltpu.VMEM((n_obs,), jnp.int32),
            pltpu.VMEM((n_obs,), jnp.int32),
            pltpu.VMEM((n_obs,), f32),
            pltpu.VMEM((n_obs,), f32),
            pltpu.VMEM((n_obs, LANES), f32),
            pltpu.VMEM((lats - NEAR, members, F, rows, LANES), f32),
            pltpu.SemaphoreType.DMA((7,)),
        ],
        compiler_params=pltpu.CompilerParams(vmem_limit_bytes=24 * MIB),
        cost_estimate=pl.CostEstimate(
            flops=4 * devices * rows * n_obs * LANES, bytes_accessed=1 << 20, transcendentals=0
        ),
    )(
        obs_count.reshape(1, 1),
        *(
            pltpu.with_memory_space_constraint(x, pltpu.HBM)
            for x in (
                obs_dest.reshape(1, n_obs),
                obs_cell,
                obs_offset,
                departure,
                obs_rinv,
                obs_weights,
            )
        )
    )
    far, near = list(messages[:F]), list(messages[F:])
    far = [to_field(far[q], q, members) for q in range(F)]
    late = [
        along_lat(jnp.stack([part[d - NEAR] for part in far]), d)
        for d in reversed(range(NEAR, lats))
    ]
    near = near[:1] + [along_lat(near[d], d) for d in range(1, NEAR)]
    near = [to_field(jnp.stack([part[q] for part in near]), q, members) for q in range(F)]
    zonal_high, zonal_low, vert_both = call(
        functools.partial(prepare_kernel, members, lon_cols),
        [
            jax.ShapeDtypeStruct((members * share, all_lons), bf16),
            jax.ShapeDtypeStruct((members * share, all_lons), bf16),
            jax.ShapeDtypeStruct((2 * LEV, 2 * LEV), bf16),
        ],
        2,
        scratch=[pltpu.VMEM(zonal_factor.shape, f32)],
        nbytes=2 << 20,
    )(zonal_factor, vert_factor)
    early = call(
        functools.partial(early_kernel, capacity),
        jax.ShapeDtypeStruct((blocks, columns, LEV), f32),
        F,
        vmem=24,
        flops=4 * blocks * columns * NEAR * F * rows * LEV,
        nbytes=2 << 20,
    )(*near)
    partial = jax.ShapeDtypeStruct((share, wide), f32)
    half_vertical = jax.ShapeDtypeStruct((all_lons, wide), bf16)
    high, low, *partials = call(
        functools.partial(late_kernel, capacity, lon_cols, len(late)),
        [half_vertical] * 2 + [partial] * (members - 1),
        4 + len(late),
        vmem=24,
        flops=6 * members * share * all_lons * wide,
        nbytes=2 << 20,
    )(*late, early, zonal_high, zonal_low, vert_both)
    others = [to_member(partials[e - 1], e, members) for e in range(1, members)]
    own = call(
        own_kernel, partial, 4, flops=6 * share * all_lons * wide, nbytes=1 << 20
    )(zonal_high, zonal_low, high, low)
    products = call(
        functools.partial(sum_kernel, lon_cols),
        [jax.ShapeDtypeStruct((lon_cols, wide), f32)] * F,
        members,
        nbytes=1 << 20,
    )(own, *others)
    parts = [to_field(products[q], q, members) for q in range(F)]
    out = ()
    for distances in ((0, 1), (2, 3)):
        count = len(distances)
        out = (
            pl.pallas_call(
                functools.partial(finish_kernel, members, distances),
                out_shape=jax.ShapeDtypeStruct(control.shape, f32),
                in_specs=[pl.BlockSpec(memory_space=pltpu.VMEM)] * (1 + count)
                + [pl.BlockSpec(memory_space=pltpu.HBM)] * len(out),
                out_specs=pl.BlockSpec(memory_space=pltpu.HBM),
                scratch_shapes=[
                    pltpu.VMEM((count, lat_rows, lon_cols, LEV), f32),
                    pltpu.SemaphoreType.DMA((count,)),
                ],
                input_output_aliases={1 + count: 0} if out else {},
                compiler_params=pltpu.CompilerParams(vmem_limit_bytes=24 * MIB),
                cost_estimate=pl.CostEstimate(
                    flops=0, bytes_accessed=count << 19, transcendentals=0
                ),
            )(control, *(parts[q] for q in distances), *out),
        )
    return out[0]


def solution(mesh):
    return jax.shard_map(
        per_device,
        mesh=mesh,
        in_specs=(
            P("lat", "lon", None),
            P(),
            P(),
            P(("lat", "lon"), None),
            P(("lat", "lon")),
            P(("lat", "lon")),
            P(("lat", "lon")),
            P(("lat", "lon")),
            P(("lat", "lon")),
            P(("lat", "lon"), None),
        ),
        out_specs=P("lat", "lon", None),
        check_vma=False,
    )
```

```python
import functools

import jax
import jax.numpy as jnp
from jax import lax
from jax.experimental import pallas as pl
from jax.experimental.pallas import tpu as pltpu
from jax.sharding import PartitionSpec as P

F = 4
LEV = 128
KW = 32
LANES = 128
SUBLANES = 8
GROUPS = LANES // KW
NEAR = 2
MIB = 1 << 20


def iota(shape, axis):
    return lax.broadcasted_iota(jnp.int32, shape, axis)


def split(x):
    high = x.astype(jnp.bfloat16)
    return high, (x - high.astype(jnp.float32)).astype(jnp.bfloat16)


def dot(a, b):
    return jnp.dot(a, b, preferred_element_type=jnp.float32)


def one_hot(labels, size):
    hit = iota((size, labels.shape[1]), 0).astype(jnp.bfloat16) == labels.astype(jnp.bfloat16)
    return jnp.where(hit, jnp.bfloat16(1), jnp.bfloat16(0))


def message_rows(capacity):
    parts = -(-capacity // KW)
    return parts, -(-(capacity + 2 * parts) // SUBLANES) * SUBLANES


def pack_kernel(members, capacity, lats, *refs):
    sources, far, near = refs[:7], refs[7 : 7 + F], refs[7 + F : 7 + F + NEAR]
    held, by_field, arrived = refs[7 + F + NEAR : -2], refs[-2], refs[-1]
    loads = [
        pltpu.make_async_copy(source, target, arrived.at[i])
        for i, (source, target) in enumerate(zip(sources, held))
    ]
    for i in (1, 6, 0, 2, 3, 4, 5):
        loads[i].start()
    count, dest, cell, offset, departure, rinv, weights = held
    n = weights.shape[0]
    rows = far[0].shape[2]
    lons = F * members
    devices = lats * lons
    field = lax.axis_index("lon") // members
    parts, _ = message_rows(capacity)
    quads = devices // GROUPS
    chunks = n // LANES
    loads[1].wait()
    lat = lax.axis_index("lat")
    band = dest[...] // lons ^ lat
    dest_row = (band ^ ((band & lat & 2) >> 1)) * lons + lax.rem(dest[...], lons)
    hits = [
        iota((devices, LANES), 0) == dest_row[:, c * LANES : (c + 1) * LANES] for c in range(chunks)
    ]
    stacked = jnp.concatenate([hit.astype(jnp.bfloat16) for hit in hits], axis=0)
    before = (iota((LANES, 2 * LANES), 0) < iota((LANES, 2 * LANES), 1)).astype(jnp.bfloat16)
    counts = dot(stacked, before)
    carry = jnp.zeros((devices, LANES), jnp.float32)
    ranks = []
    for c in range(chunks):
        part = counts[c * devices : (c + 1) * devices]
        ranks.append(
            jnp.sum(jnp.where(hits[c], part[:, :LANES] + carry, 0.0), axis=0, keepdims=True)
        )
        carry = carry + part[:, LANES:]
    rank = jnp.concatenate(ranks, axis=1).astype(jnp.int32)
    group = dest_row & (GROUPS - 1)
    quad = dest_row >> (GROUPS.bit_length() - 1)
    slot = group * rows + rank
    lane = group * KW + (rank & (KW - 1))
    piece = rank >> (KW.bit_length() - 1)
    for i in (0, 2, 3, 4, 5):
        loads[i].wait()
    cell_row, offset_row = cell[...].reshape(1, n), offset[...].reshape(1, n)
    live = iota((1, n), 1) < count[0, 0]
    scaled = jnp.where(
        live, rinv[...].reshape(1, n) * departure[...].reshape(1, n), jnp.float32(0.0)
    )
    columns = jnp.concatenate(
        [scaled, offset_row.astype(jnp.float32), jnp.zeros((SUBLANES - 2, n), jnp.float32)], axis=0
    ).T
    lane_id = iota((n, LANES), 1)
    label_rows = []
    for p in range(parts):
        for label in (cell_row, offset_row):
            mine = (iota((quads, n), 0) == quad) & (piece == p)
            label_rows.append(jnp.where(mine, label.astype(jnp.float32), 0.0))
    labels = lax.dot_general(
        jnp.concatenate(label_rows, axis=0).astype(jnp.bfloat16),
        one_hot(lane, LANES),
        (((1,), (1,)), ((), ())),
        preferred_element_type=jnp.float32,
    )
    source = (lane_id & -KW) | ((lane_id - columns[:, 1:2].astype(jnp.int32)) & (KW - 1))
    loads[6].wait()
    turned = jnp.take_along_axis(weights[...], source, axis=1, mode="promise_in_bounds")
    high, low = split(turned * columns[:, 0:1])
    pieces = jnp.concatenate([high, low], axis=1)
    even = iota((rows, LANES), 1) & KW == 0
    lower = iota((rows, LANES), 1) < LANES // 2
    size = GROUPS * rows
    tail = capacity // SUBLANES * SUBLANES
    row_id = iota((rows - tail, LANES), 0) + tail
    order = (*range(NEAR, lats), *reversed(range(NEAR)))
    hits = jnp.concatenate(
        [
            one_hot(jnp.where(quad == distance * members + half, slot, -1), size)
            for distance in order
            for half in range(members)
        ],
        axis=0,
    )
    both = dot(hits, pieces)
    for step, distance in enumerate(order):
        for half in range(members):
            at = (step * members + half) * size
            picked = both[at : at + size, :LANES] + both[at : at + size, LANES:]
            blocks = [picked[g * rows : (g + 1) * rows] for g in range(GROUPS)]
            pairs = [
                part
                for i in (0, 2)
                for part in (
                    jnp.where(even, blocks[i], pltpu.roll(blocks[i + 1], KW, 1)),
                    jnp.where(even, pltpu.roll(blocks[i], LANES - KW, 1), blocks[i + 1]),
                )
            ]
            fields = [
                jnp.where(lower, pairs[0], pltpu.roll(pairs[2], LANES // 2, 1)),
                jnp.where(lower, pairs[1], pltpu.roll(pairs[3], LANES // 2, 1)),
                jnp.where(lower, pltpu.roll(pairs[0], LANES // 2, 1), pairs[2]),
                jnp.where(lower, pltpu.roll(pairs[1], LANES // 2, 1), pairs[3]),
            ]
            extra = jnp.zeros((rows - tail, LANES), jnp.float32)
            for i in range(2 * parts):
                k = i * quads + distance * members + half
                extra = jnp.where(row_id == capacity + i, labels[k : k + 1], extra)
            for f in range(F):
                message = jnp.concatenate([fields[f][:tail], fields[f][tail:] + extra], axis=0)
                if distance < NEAR:
                    near[distance][field ^ f, half] = message
                else:
                    by_field[distance - NEAR, half, f] = message
            if distance >= NEAR:
                for q in range(F):
                    far[q][distance - NEAR, half] = by_field[distance - NEAR, half, field ^ q]


def prepare_kernel(members, lon_cols, zonal, vert, zonal_high, zonal_low, vert_both, turned):
    position = lax.axis_index("lon")
    f, h = position // members, lax.rem(position, members)
    turned[...] = zonal[...].T
    for e in range(members):
        for q in range(F):
            block = (f ^ q) * members + lax.rem(h + e, members)
            part = turned[pl.ds(pl.multiple_of(block * lon_cols, lon_cols), lon_cols), :]
            at = slice((e * F + q) * lon_cols, (e * F + q + 1) * lon_cols)
            zonal_high[at], zonal_low[at] = split(part)
    high, low = split(vert[f])
    vert_both[:LEV, :LEV] = high
    vert_both[:LEV, LEV:] = low
    vert_both[LEV:, :LEV] = high
    vert_both[LEV:, LEV:] = jnp.zeros_like(low)


def scatter(pieces, half, capacity, columns):
    rows = pieces[0].shape[0]
    count = len(pieces)
    slots = -(-count * rows // (2 * LANES)) * 2 * LANES
    parts, _ = message_rows(capacity)
    row_id, lane_id = iota((rows, LANES), 0), iota((rows, LANES), 1)
    piece_id = row_id >> (KW.bit_length() - 1)
    diagonal = ((lane_id & (KW - 1)) == (row_id & (KW - 1))) & (row_id < capacity)
    empty = jnp.where((row_id >= capacity) & ((lane_id & (KW - 1)) == 0), -1.0, 0.0)
    labels = []
    for piece in pieces:
        cell, offset = empty, jnp.zeros((rows, LANES), jnp.float32)
        for p in range(parts):
            mine = diagonal & (piece_id == p)
            at = capacity + 2 * p
            cell = jnp.where(mine, piece[at : at + 1], cell)
            offset = jnp.where(mine, piece[at + 1 : at + 2], offset)
        labels.append(jnp.concatenate([cell, offset], axis=1))
    spare = slots - count * rows
    if spare:
        pieces = pieces + [jnp.zeros((spare, LANES), jnp.float32)]
        labels.append(jnp.full((spare, 2 * LANES), -1.0, jnp.float32))
    picker = (
        iota((2 * GROUPS, 2 * LANES), 0) == iota((2 * GROUPS, 2 * LANES), 1) >> (KW.bit_length() - 1)
    ).astype(jnp.bfloat16)
    along = (((1,), (1,)), ((), ()))
    label_rows = lax.dot_general(
        picker,
        jnp.concatenate(labels, axis=0).astype(jnp.bfloat16),
        along,
        preferred_element_type=jnp.float32,
    ).astype(jnp.bfloat16)
    high, low = split(jnp.concatenate(pieces, axis=0).T)
    middle = iota((LEV, slots), 0).astype(jnp.bfloat16) - jnp.bfloat16((KW - 1) / 2)
    sums = []
    for g in range(GROUPS):
        at = slice(g * KW, (g + 1) * KW)
        inside = jnp.abs(middle - label_rows[GROUPS + g : GROUPS + g + 1]) < jnp.bfloat16(KW / 2)
        placed = jnp.concatenate(
            [
                jnp.where(inside, jnp.concatenate([piece[at]] * (LEV // KW), axis=0), jnp.bfloat16(0))
                for piece in (high, low)
            ],
            axis=0,
        )
        both = lax.dot_general(
            one_hot(label_rows[g : g + 1], columns),
            placed,
            along,
            preferred_element_type=jnp.float32,
        )
        sums.append(both[:, :LEV] + both[:, LEV:])
    return sums


def early_kernel(capacity, *refs):
    received, out = refs[:-1], refs[-1]
    halves, columns = received[0].shape[1], out.shape[1]
    for half in range(halves):
        pieces = [ref[k, half] for ref in received for k in range(ref.shape[0])]
        for g, total in enumerate(scatter(pieces, half, capacity, columns)):
            out[half * GROUPS + g] = total


def late_kernel(capacity, lon_cols, count, *refs):
    received = refs[:count]
    early, zonal_high, zonal_low, vert_both, high_out, low_out, *partials = refs[count:]
    halves, columns = received[0].shape[1], early.shape[1]
    for half in range(halves):
        pieces = [ref[k, half] for ref in received for k in range(ref.shape[0])]
        for g, total in enumerate(scatter(pieces, half, capacity, columns)):
            block = half * GROUPS + g
            adjoint_high, adjoint_low = split(early[block] + total)
            both = dot(jnp.concatenate([adjoint_high, adjoint_low], axis=1), vert_both[...])
            vertical = both[:, :LEV] + both[:, LEV:]
            high, low = split(vertical)
            for a in range(columns // lon_cols):
                at = slice(block * lon_cols, (block + 1) * lon_cols)
                rows = slice(a * lon_cols, (a + 1) * lon_cols)
                high_out[at, a * LEV : (a + 1) * LEV] = high[rows]
                low_out[at, a * LEV : (a + 1) * LEV] = low[rows]
    for e, partial in enumerate(partials, 1):
        partial[...] = zonal_product(e, zonal_high, zonal_low, high_out, low_out, partial.shape[0])


def zonal_product(e, zonal_high, zonal_low, high, low, size):
    at = slice(e * size, (e + 1) * size)
    first = dot(zonal_high[at], high[...]) + dot(zonal_low[at], high[...])
    return first + dot(zonal_high[at], low[...])


def own_kernel(zonal_high, zonal_low, high, low, out):
    out[...] = zonal_product(0, zonal_high, zonal_low, high, low, out.shape[0])


def sum_kernel(lon_cols, *refs):
    terms, outs = refs[:-F], refs[-F:]
    for q in range(F):
        at = slice(q * lon_cols, (q + 1) * lon_cols)
        total = terms[0][at]
        for term in terms[1:]:
            total = total + term[at]
        outs[q][...] = total


def finish_kernel(members, distances, *refs):
    count = len(distances)
    control, parts = refs[0], refs[1 : 1 + count]
    out, held, sent = refs[-3:]
    field = lax.axis_index("lon") // members
    copies = []
    for i, q in enumerate(distances):
        at = pl.ds(pl.multiple_of((field ^ q) * LEV, LEV), LEV)
        for a in range(control.shape[0]):
            held[i, a] = control[a, :, at] + parts[i][:, a * LEV : (a + 1) * LEV]
        copies.append(pltpu.make_async_copy(held.at[i], out.at[:, :, at], sent.at[i]))
        copies[-1].start()
    for copy in copies:
        copy.wait()


def call(kernel, out_shape, n_in, vmem=24, flops=0, nbytes=0, scratch=()):
    one = pl.BlockSpec(memory_space=pltpu.VMEM)
    return pl.pallas_call(
        kernel,
        out_shape=out_shape,
        in_specs=[one] * n_in,
        out_specs=[one] * len(out_shape) if isinstance(out_shape, (list, tuple)) else one,
        scratch_shapes=list(scratch),
        compiler_params=pltpu.CompilerParams(vmem_limit_bytes=vmem * MIB),
        cost_estimate=pl.CostEstimate(flops=flops, bytes_accessed=nbytes, transcendentals=0),
    )


def along_lat(x, d):
    lats = lax.axis_size("lat")
    return lax.ppermute(x, "lat", [(i, i ^ d ^ ((i & d & 2) >> 1)) for i in range(lats)])


def to_field(x, q, members):
    if q == 0:
        return x
    lons = lax.axis_size("lon")
    return lax.ppermute(
        x, "lon", [(i, (i // members ^ q) * members + i % members) for i in range(lons)]
    )


def to_member(x, e, members):
    lons = lax.axis_size("lon")
    return lax.ppermute(
        x, "lon", [(i, i // members * members + (i + e) % members) for i in range(lons)]
    )


def per_device(
    control,
    vert_factor,
    zonal_factor,
    obs_dest,
    obs_cell,
    obs_offset,
    obs_count,
    departure,
    obs_rinv,
    obs_weights,
):
    lats = lax.axis_size("lat")
    lons = lax.axis_size("lon")
    devices = lats * lons
    members = lons // F
    n_obs = obs_cell.shape[0]
    capacity = max(2, 3 * n_obs // (2 * devices))
    _, rows = message_rows(capacity)
    lat_rows, lon_cols, _ = control.shape
    columns = lat_rows * lon_cols
    blocks = lons
    all_lons = lons * lon_cols
    share = F * lon_cols
    wide = lat_rows * LEV
    f32, bf16 = jnp.float32, jnp.bfloat16
    far_messages = jax.ShapeDtypeStruct((lats - NEAR, members, rows, LANES), f32)
    near_messages = jax.ShapeDtypeStruct((F, members, rows, LANES), f32)
    messages = pl.pallas_call(
        functools.partial(pack_kernel, members, capacity, lats),
        out_shape=[far_messages] * F + [near_messages] * NEAR,
        in_specs=[pl.BlockSpec(memory_space=pltpu.HBM)] * 7,
        out_specs=[pl.BlockSpec(memory_space=pltpu.VMEM)] * (F + NEAR),
        scratch_shapes=[
            pltpu.SMEM((1, 1), jnp.int32),
            pltpu.VMEM((1, n_obs), jnp.int32),
            pltpu.VMEM((n_obs,), jnp.int32),
            pltpu.VMEM((n_obs,), jnp.int32),
            pltpu.VMEM((n_obs,), f32),
            pltpu.VMEM((n_obs,), f32),
            pltpu.VMEM((n_obs, LANES), f32),
            pltpu.VMEM((lats - NEAR, members, F, rows, LANES), f32),
            pltpu.SemaphoreType.DMA((7,)),
        ],
        compiler_params=pltpu.CompilerParams(vmem_limit_bytes=24 * MIB),
        cost_estimate=pl.CostEstimate(
            flops=4 * devices * rows * n_obs * LANES, bytes_accessed=1 << 20, transcendentals=0
        ),
    )(
        obs_count.reshape(1, 1),
        *(
            pltpu.with_memory_space_constraint(x, pltpu.HBM)
            for x in (
                obs_dest.reshape(1, n_obs),
                obs_cell,
                obs_offset,
                departure,
                obs_rinv,
                obs_weights,
            )
        )
    )
    far, near = list(messages[:F]), list(messages[F:])
    far = [to_field(far[q], q, members) for q in range(F)]
    late = [
        along_lat(jnp.stack([part[d - NEAR] for part in far]), d)
        for d in reversed(range(NEAR, lats))
    ]
    near = near[:1] + [along_lat(near[d], d) for d in range(1, NEAR)]
    near = [to_field(jnp.stack([part[q] for part in near]), q, members) for q in range(F)]
    zonal_high, zonal_low, vert_both = call(
        functools.partial(prepare_kernel, members, lon_cols),
        [
            jax.ShapeDtypeStruct((members * share, all_lons), bf16),
            jax.ShapeDtypeStruct((members * share, all_lons), bf16),
            jax.ShapeDtypeStruct((2 * LEV, 2 * LEV), bf16),
        ],
        2,
        scratch=[pltpu.VMEM(zonal_factor.shape, f32)],
        nbytes=2 << 20,
    )(zonal_factor, vert_factor)
    early = call(
        functools.partial(early_kernel, capacity),
        jax.ShapeDtypeStruct((blocks, columns, LEV), f32),
        F,
        vmem=24,
        flops=4 * blocks * columns * NEAR * F * rows * LEV,
        nbytes=2 << 20,
    )(*near)
    partial = jax.ShapeDtypeStruct((share, wide), f32)
    half_vertical = jax.ShapeDtypeStruct((all_lons, wide), bf16)
    high, low, *partials = call(
        functools.partial(late_kernel, capacity, lon_cols, len(late)),
        [half_vertical] * 2 + [partial] * (members - 1),
        4 + len(late),
        vmem=24,
        flops=6 * members * share * all_lons * wide,
        nbytes=2 << 20,
    )(*late, early, zonal_high, zonal_low, vert_both)
    others = [to_member(partials[e - 1], e, members) for e in range(1, members)]
    own = call(
        own_kernel, partial, 4, flops=6 * share * all_lons * wide, nbytes=1 << 20
    )(zonal_high, zonal_low, high, low)
    products = call(
        functools.partial(sum_kernel, lon_cols),
        [jax.ShapeDtypeStruct((lon_cols, wide), f32)] * F,
        members,
        nbytes=1 << 20,
    )(own, *others)
    parts = [to_field(products[q], q, members) for q in range(F)]
    out = ()
    for distances in ((0, 1), (2, 3)):
        count = len(distances)
        out = (
            pl.pallas_call(
                functools.partial(finish_kernel, members, distances),
                out_shape=jax.ShapeDtypeStruct(control.shape, f32),
                in_specs=[pl.BlockSpec(memory_space=pltpu.VMEM)] * (1 + count)
                + [pl.BlockSpec(memory_space=pltpu.HBM)] * len(out),
                out_specs=pl.BlockSpec(memory_space=pltpu.HBM),
                scratch_shapes=[
                    pltpu.VMEM((count, lat_rows, lon_cols, LEV), f32),
                    pltpu.SemaphoreType.DMA((count,)),
                ],
                input_output_aliases={1 + count: 0} if out else {},
                compiler_params=pltpu.CompilerParams(vmem_limit_bytes=24 * MIB),
                cost_estimate=pl.CostEstimate(
                    flops=0, bytes_accessed=count << 19, transcendentals=0
                ),
            )(control, *(parts[q] for q in distances), *out),
        )
    return out[0]


def solution(mesh):
    return jax.shard_map(
        per_device,
        mesh=mesh,
        in_specs=(
            P("lat", "lon", None),
            P(),
            P(),
            P(("lat", "lon"), None),
            P(("lat", "lon")),
            P(("lat", "lon")),
            P(("lat", "lon")),
            P(("lat", "lon")),
            P(("lat", "lon")),
            P(("lat", "lon"), None),
        ),
        out_specs=P("lat", "lon", None),
        check_vma=False,
    )
```
